256 devices in a mesh: doc: 32 (over y, z), tok: 8 (over x, core).
Axes of the slice: x: 4, y: 4, z: 8, core: 2. Of those that a mesh axis runs over, the one named last changes fastest.
Arguments:
- query_states: bfloat16 [256, 32, 1024], P('doc', 'tok'), may hold values from -6 to 6
- proj_weight: bfloat16 [1024, 128], replicated, may hold values from -0.1875 to 0.1875
- doc_vectors: bfloat16 [32768, 128, 128], P('doc', 'tok'), may hold values from -0.52734375 to 0.52734375
- document_token_length: int32 [32768], P('doc'), may hold values from 1 to 128
- candidates: int32 [256, 256], P('doc'), may hold values from 0 to 32767, as said below
Outputs:
- scores: float32 [256, 256], P('doc')
The draws below stay inside these ranges and needn't reach their ends.
Inputs may be any that keep to these rules, and one draw needn't show every extreme that they name: `candidates`: write shard(e) = id // 1024. Among the 2048 entries of the queries held at one position along doc, one shard, the same for every index of doc, is named by exactly 128 entries, and each other shard by the floor or the ceiling of 1920 / 31 entries. Ids may repeat within a query.
All inputs are finite; a program needn't handle non-finite values.
Results may differ from the reference program's by a relative error of at most 0.0003.
Values may be sent and summed in bfloat16 or wider, within the bound.
A program may use at most 64 MiB of HBM per device.

```python
import jax
import jax.numpy as jnp
from jax import lax

D = 1024
DIM = 128
QT = 32
DTOK = 128
CANDS = 256
Q_DEV = 8
DOCS_PER_INDEX = 1024
QUERIES = 256
NDOCS = 32768
CAP = 128
N_DOC = 32


def draw_candidates(key, part):
    key = jax.random.fold_in(key, 11)
    entries = Q_DEV * CANDS
    hot_shard = jax.random.randint(jax.random.fold_in(key, 1), (), 0, N_DOC)
    block_keys = jax.random.split(jax.random.fold_in(key, 2), N_DOC)

    def one_block(block_key):
        first_key, second_key = jax.random.split(block_key)
        position = jnp.arange(entries, dtype=jnp.int32)
        others = (hot_shard + 1 + (position - CAP) % (N_DOC - 1)) % N_DOC
        shard_of = jnp.where(position < CAP, hot_shard, others)
        shard_of = jax.random.permutation(first_key, shard_of)
        local_id = jax.random.randint(second_key, (entries,), 0, DOCS_PER_INDEX)
        return (shard_of * DOCS_PER_INDEX + local_id).astype(jnp.int32).reshape(Q_DEV, CANDS)
    return jax.vmap(one_block)(block_keys).reshape(Q_DEV * N_DOC, CANDS)


def with_ends(array, own_key, least, largest):
    longest = array.shape.index(max(array.shape))
    spots = []
    for shift in (0, 1):
        where = [jax.random.randint(jax.random.fold_in(own_key, axis), (), 0, length) for axis, length in enumerate(array.shape)]
        where[longest] = (where[longest] + shift) % array.shape[longest]
        spots.append(tuple(where))
    return array.at[spots[0]].set(least).at[spots[1]].set(largest)


def steps_of(rng, shape, cuts, least, top_value):
    def one(dim, blocks):
        heights = jax.random.uniform(jax.random.fold_in(jax.random.fold_in(rng, 6), dim), (blocks,), jnp.float32, least / len(cuts), top_value / len(cuts))
        return jnp.repeat(jnp.exp(heights), shape[dim] // blocks).reshape((-1,) + (1,) * (len(shape) - dim - 1))

    loudness = one(*cuts[0])
    for cut in cuts[1:]:
        loudness = loudness * one(*cut)
    return loudness


def centred(own_key, extent, spread, limit, pieces=(), kind=jnp.bfloat16):
    values = spread * jax.random.normal(own_key, extent, jnp.float32)
    if pieces:
        values = values * steps_of(own_key, extent, pieces, -0.22, 0.18)
    return jnp.clip(values, -limit, limit).astype(kind)


def setup_inputs(seed: int = 0) -> dict:
    splits = jax.random.split(jax.random.key(seed), 6)
    return {
        "query_states": centred(splits[0], (QUERIES, QT, D), 1.0, 6.0, ((0, 32), (1, 8))),
        "proj_weight": centred(splits[1], (D, DIM), D ** -0.5, 0.1875),
        "doc_vectors": centred(splits[2], (NDOCS, DTOK, DIM), (DIM ** -0.5), 0.52734375, ((0, 32), (1, 8))),
        "document_token_length": with_ends(jax.random.randint(splits[3], (NDOCS,), 1, DTOK + 1), jax.random.fold_in(splits[3], 1), 1, DTOK).astype(jnp.int32),
        "candidates": draw_candidates(jax.random.fold_in(splits[5], 71), 0),
    }


def reference(query_states, proj_weight, doc_vectors, document_token_length, candidates):
    proj = jnp.einsum('qtd,de->qte', query_states.astype(jnp.float32), proj_weight.astype(jnp.float32))
    unit = (proj / jnp.sqrt(lax.optimization_barrier(jnp.sum(proj * proj, axis=-1, keepdims=True)) + 1e-06)).astype(jnp.bfloat16)
    positions = jnp.arange(DTOK, dtype=jnp.int32)

    def score_query(pair):
        query_embeddings, cand_ids = pair
        chosen = doc_vectors[cand_ids].astype(jnp.float32)
        live = positions[None, :] < document_token_length[cand_ids][:, None]
        similarity_scores = jnp.einsum('ic,nkc->nik', query_embeddings.astype(jnp.float32), chosen)
        similarity_scores = jnp.where(live[:, None, :], similarity_scores, jnp.float32(-1e+30))
        return lax.optimization_barrier(jnp.sum(lax.optimization_barrier(jnp.max(similarity_scores, axis=2)), axis=1))
    return lax.map(score_query, (unit, candidates))
```

```python
import functools

import jax
import jax.numpy as jnp
from jax import lax
from jax.experimental import pallas as pl
from jax.experimental.pallas import tpu as pltpu
from jax.sharding import PartitionSpec as P

MESH = pl.DeviceIdType.MESH
F32, BF16, I32 = jnp.float32, jnp.bfloat16, jnp.int32
NT = (((1,), (1,)), ((), ()))
AHEAD = 8


def iota(shape, dim):
    return lax.broadcasted_iota(I32, shape, dim)


def kernel(
    ny, nz, nt, docs_hbm, qs_hbm, w_hbm, len_ref, cand_ref, out_ref,
    docs, qs, w, ublk, qall, lists_out, lists_in, lists, expand, lens_in, onehots, ranks,
    best, inbox, sums, table, table2,
    in_sem, a_send, a_recv, l_send, l_recv, q_recv, y_send, zp_send, zm_send, sib_send,
    m_send, m_recv, t_send, t_recv, s_sem,
):
    no = ny * nz
    d, t = lax.axis_index("doc"), lax.axis_index("tok")
    y, z, c = d // nz, d % nz, t % 2
    sibling = t + 1 - 2 * c
    nq, cands = cand_ref.shape
    ndocs = docs.shape[0]
    slots = docs.shape[1]
    shift = ndocs.bit_length() - 1
    qrows = nq * (ublk.shape[1] // nq) * nt
    cap = lists_in.shape[2]

    loads = [
        pltpu.make_async_copy(src, dst, in_sem.at[i])
        for i, (src, dst) in enumerate(((qs_hbm, qs), (w_hbm, w), (docs_hbm, docs)))
    ]
    for load in loads:
        load.start()

    barrier = pltpu.get_barrier_semaphore()

    def greet_tok(p, carry):
        pl.semaphore_signal(barrier, inc=1, device_id={"doc": d, "tok": (t + p) % nt}, device_id_type=MESH)
        return carry

    def greet_doc(p, carry):
        pl.semaphore_signal(barrier, inc=1, device_id={"doc": (d + p) % no, "tok": t}, device_id_type=MESH)
        return carry

    lax.fori_loop(1, nt, greet_tok, 0)
    lax.fori_loop(1, no, greet_doc, 0)

    def send(src, dst, ssem, rsem, doc, tok):
        return pltpu.make_async_remote_copy(
            src_ref=src, dst_ref=dst, send_sem=ssem, recv_sem=rsem,
            device_id={"doc": doc, "tok": tok}, device_id_type=MESH,
        )

    cand = cand_ref[...]
    shard_rows = []
    for q in range(nq):
        shard_rows.append((iota((no, cands), 0) == (cand[q : q + 1] >> shift)).astype(F32))
    before = (iota((cands, cands), 0) < iota((cands, cands), 1)).astype(BF16)
    prefix = jnp.dot(
        jnp.concatenate(shard_rows, axis=0).astype(BF16), before, preferred_element_type=F32
    )
    base = jnp.zeros((no, 1), F32)
    coded = jnp.zeros((2 * no, cap), F32)
    for q in range(nq):
        mine = shard_rows[q]
        rank = jnp.sum(mine * (prefix[no * q : no * (q + 1)] + base), axis=0, keepdims=True)
        base = base + jnp.sum(mine, axis=1, keepdims=True)
        ranks[q] = rank
        onehots[q] = mine.astype(BF16)
        local = cand[q : q + 1] & (ndocs - 1)
        high = (local >> 8) + (ndocs >> 8) * q
        low = local & 255
        rank_rows = (iota((cap, cands), 0).astype(F32) == rank).astype(BF16)
        lhs = jnp.concatenate([mine * high.astype(F32), mine * low.astype(F32)], axis=0)
        coded = coded + lax.dot_general(lhs.astype(BF16), rank_rows, NT, preferred_element_type=F32)
    packed = coded[:no].astype(I32) * 256 + coded[no:].astype(I32)
    for s in range(no):
        lists_out[s] = packed[s : s + 1]
    lists_in[d] = lists_out[d]

    loads[0].wait()
    loads[1].wait()
    proj = jnp.dot(qs[...], w[...], preferred_element_type=F32)
    unit = proj * lax.rsqrt(jnp.sum(proj * proj, axis=-1, keepdims=True) + 1e-06)
    ublk[t] = unit.astype(BF16)

    pl.semaphore_wait(barrier, nt - 1 + no - 1)

    def send_unit(p):
        return send(ublk.at[t], ublk.at[t], a_send.at[p], a_recv.at[t], d, (t + p) % nt)

    def send_list(p):
        s = (d + p) % no
        return send(lists_out.at[s], lists_in.at[d], l_send.at[p], l_recv.at[d], s, t)

    def start_of(make):
        def body(p, carry):
            make(p).start()
            return carry

        return body

    def sent_of(make):
        def body(p, carry):
            make(p).wait_send()
            return carry

        return body

    lax.fori_loop(1, nt, start_of(send_unit), 0)
    lax.fori_loop(1, no, start_of(send_list), 0)

    def unit_arrived(p, carry):
        src = (t + p) % nt
        send(ublk.at[src], ublk.at[src], a_send.at[0], a_recv.at[src], d, src).wait_recv()
        return carry

    lax.fori_loop(1, nt, unit_arrived, 0)

    per = ublk.shape[1] // nq
    row, col = iota((qrows, qrows), 0), iota((qrows, qrows), 1)
    from_row = ((row // per) % nt) * (per * nq) + (row // (per * nt)) * per + row % per
    order = (from_row == col).astype(BF16)
    mixed = jnp.concatenate([ublk[i] for i in range(nt)], axis=0)
    sorted_rows = jnp.dot(order, mixed, preferred_element_type=F32).astype(BF16)
    half = qrows // 2
    qall[d, 0] = sorted_rows[:half]
    qall[d, 1] = sorted_rows[half:]

    def send_y(p):
        return send(qall.at[d, c], qall.at[d, c], y_send.at[p], q_recv.at[d, c], ((y + p) % ny) * nz + z, t)

    lax.fori_loop(1, ny, start_of(send_y), 0)

    far = nz // 2

    def place(j):
        first, last = j < ny, j >= no - ny
        mid = j - ny
        step = jnp.where(first, 0, mid // (2 * ny) + 1)
        r = mid % (2 * ny)
        yy = jnp.where(first, j, jnp.where(last, j - (no - ny), r // 2))
        back = jnp.where(first, 0, jnp.where(last, yy % 2, r % 2))
        zz = (z + nz + jnp.where(back == 0, -step, step)) % nz
        return step, back, yy, yy * nz + zz

    def copies(j):
        step, back, yy, o = place(j)
        own = o == d
        onward = (step < far - 1) | ((step == far - 1) & (yy % 2 == back))
        plus = (step == 0) | ((back == 0) & onward)
        minus = (step == 0) | ((back == 1) & onward)
        block, arrival = qall.at[o, c], q_recv.at[o, c]
        return (
            own, plus, minus, o,
            send(block, block, zp_send.at[j], arrival, y * nz + (z + 1) % nz, t),
            send(block, block, zm_send.at[j], arrival, y * nz + (z + nz - 1) % nz, t),
            send(block, block, sib_send.at[j], arrival, d, sibling),
        )

    def forward(j):
        own, plus, minus, o, to_plus, to_minus, to_sibling = copies(j)

        @pl.when(jnp.logical_not(own))
        def _():
            to_sibling.wait_recv()

        @pl.when(plus)
        def _():
            to_plus.start()

        @pl.when(minus)
        def _():
            to_minus.start()

        @pl.when(jnp.logical_not(own))
        def _():
            to_sibling.start()

    def list_arrived(p, carry):
        src = (d + p) % no
        send(lists_in.at[src], lists_in.at[src], l_send.at[0], l_recv.at[src], src, t).wait_recv()
        return carry

    def forward_body(j, carry):
        forward(j)
        return carry

    ahead = min(AHEAD, no)
    lax.fori_loop(0, ahead, forward_body, 0)
    lax.fori_loop(1, no, list_arrived, 0)
    to_smem = pltpu.make_async_copy(lists_in, lists, s_sem)
    to_smem.start()

    for s in range(no):
        lens_in[s : s + 1] = lists_in[s]
    entry = lens_in[...]
    doc_id = entry & (ndocs - 1)
    lanes = len_ref.shape[1]
    length = jnp.zeros(entry.shape, I32)
    for r in range(len_ref.shape[0]):
        line = jnp.broadcast_to(len_ref[r : r + 1], (no, lanes))
        found = jnp.take_along_axis(line, doc_id % lanes, axis=1)
        length = jnp.where(doc_id // lanes == r, found, length)
    both = jnp.concatenate([entry >> shift, length], axis=0).astype(F32).astype(BF16)
    groups = cap // slots
    width = cap * slots
    lane_row, lane_col = iota((cap, width), 0), iota((cap, width), 1)
    pick = (lane_row == (lane_col % cap) // slots * slots + lane_col // cap).astype(BF16)
    spread = jnp.dot(both, pick, preferred_element_type=F32)
    for s in range(2 * no):
        expand[s] = spread[s : s + 1]

    loads[2].wait()
    to_smem.wait()
    position = (t * slots + iota((8, cap), 1) % slots).astype(F32)
    lane = iota((8, cap), 1)
    per_query = qrows // nq

    def merge(a, b, dist):
        keep = ((lane // dist) % 2 == 0)[None]
        a_back = pltpu.roll(a, cap - dist, 2)
        b_on = pltpu.roll(b, dist, 2)
        return jnp.maximum(jnp.where(keep, a, b_on), jnp.where(keep, a_back, b))

    def compute(j):
        o = place(j)[3]

        @pl.when(o != d)
        def _():
            other = qall.at[o, 1 - c]
            send(other, other, sib_send.at[j], q_recv.at[o, 1 - c], d, sibling).wait_recv()

        query = jnp.concatenate([qall[o, 0], qall[o, 1]], axis=0)

        def tile(v):
            parts = []
            for u in (v, v + slots // 2):
                for g in range(groups):
                    parts.append(docs[lists[o, 0, g * slots + u] & (ndocs - 1)])
            matrix = jnp.concatenate(parts, axis=0)
            sims = lax.dot_general(query, matrix, NT, preferred_element_type=F32)
            out = []
            for h, u in enumerate((v, v + slots // 2)):
                block = sims[:, h * cap : (h + 1) * cap].reshape(nq, per_query // 8, 8, cap)
                whose = jnp.broadcast_to(expand[o, :, u * cap : (u + 1) * cap], (8, cap))
                until = jnp.broadcast_to(expand[o + no, :, u * cap : (u + 1) * cap], (8, cap))
                picked = block[0]
                for q in range(1, nq):
                    picked = jnp.where((whose == q)[None], block[q], picked)
                out.append(jnp.where((position < until)[None], picked, F32(-1e30)))
            return merge(out[0], out[1], slots // 2)

        def tree(v, dist):
            if dist == slots // 2:
                return tile(v)
            return merge(tree(v, dist * 2), tree(v + dist, dist * 2), dist)

        best[j] = tree(0, 1).reshape(per_query, cap)

    def send_best(j):
        return send(best.at[j], inbox.at[j // nt, t], m_send.at[j], m_recv.at[j // nt, t], d, j % nt)

    def send_sum(m, tp):
        o = place(t + nt * m)[3]
        return (o == d) & (tp == t), send(sums.at[m], table.at[d], t_send.at[m, tp], t_recv.at[d], o, tp)

    def reduce(m):
        total = best[t + nt * m]

        def more(p, total):
            src = (t + p) % nt
            send(inbox.at[m, src], inbox.at[m, src], m_send.at[0], m_recv.at[m, src], d, src).wait_recv()
            return jnp.maximum(total, inbox[m, src])

        total = lax.fori_loop(1, nt, more, total)
        sums[m] = jnp.sum(total, axis=0, keepdims=True)

        def give(tp, carry):
            mine, copy = send_sum(m, tp)

            @pl.when(mine)
            def _():
                table[d] = sums[m]

            @pl.when(jnp.logical_not(mine))
            def _():
                copy.start()

            return carry

        lax.fori_loop(0, nt, give, 0)

    def step(j, carry):
        @pl.when(j + ahead < no)
        def _():
            forward(j + ahead)

        compute(j)

        @pl.when(j % nt != t)
        def _():
            send_best(j).start()

        @pl.when((j % nt == nt - 1) & (j >= 2 * nt - 1))
        def _():
            reduce(j // nt - 1)

        return carry

    lax.fori_loop(0, no, step, 0)
    reduce(no // nt - 1)

    def score_arrived(s, carry):
        @pl.when(jnp.logical_not((s == d) & (t == y % nt)))
        def _():
            send(table.at[s], table.at[s], t_send.at[0, 0], t_recv.at[s], s, t).wait_recv()

        return carry

    lax.fori_loop(0, no, score_arrived, 0)

    for s in range(no):
        table2[s : s + 1] = table[s]
    whole = table2[...]
    top = whole.astype(BF16).astype(F32)
    rest = whole - top
    middle = rest.astype(BF16).astype(F32)
    stacked = [top, middle, rest - middle]
    pad = 128 - 3 * no
    stacked.append(jnp.zeros((pad, cap), F32))
    turned = jnp.transpose(jnp.concatenate(stacked, axis=0)).astype(BF16)
    for q in range(nq):
        mine = onehots[q]
        select = jnp.concatenate([mine, mine, mine, jnp.zeros((pad, cands), BF16)], axis=0)
        found = jnp.dot(turned, select, preferred_element_type=F32)
        hit = iota((cap, cands), 0).astype(F32) == ranks[q]
        out_ref[q : q + 1] = jnp.sum(jnp.where(hit, found, F32(0.0)), axis=0, keepdims=True)

    lax.fori_loop(1, nt, sent_of(send_unit), 0)
    lax.fori_loop(1, no, sent_of(send_list), 0)
    lax.fori_loop(1, ny, sent_of(send_y), 0)

    def drained(j, carry):
        own, plus, minus, o, to_plus, to_minus, to_sibling = copies(j)

        @pl.when(plus)
        def _():
            to_plus.wait_send()

        @pl.when(minus)
        def _():
            to_minus.wait_send()

        @pl.when(jnp.logical_not(own))
        def _():
            to_sibling.wait_send()

        @pl.when(j % nt != t)
        def _():
            send_best(j).wait_send()

        return carry

    lax.fori_loop(0, no, drained, 0)

    def sums_left(i, carry):
        mine, copy = send_sum(i // nt, i % nt)

        @pl.when(jnp.logical_not(mine))
        def _():
            copy.wait_send()

        return carry

    lax.fori_loop(0, no, sums_left, 0)


def on_device(ny, nz, nt, query_states, proj_weight, doc_vectors, document_token_length, candidates):
    nq, per, width = query_states.shape
    ndocs, slots, dim = doc_vectors.shape
    cands = candidates.shape[1]
    no = ny * nz
    cap = 2 * nq * cands // no
    rows = nq * per
    dma = pltpu.SemaphoreType.DMA
    vmem, hbm = pl.BlockSpec(memory_space=pltpu.VMEM), pl.BlockSpec(memory_space=pl.ANY)
    return pl.pallas_call(
        functools.partial(kernel, ny, nz, nt),
        out_shape=jax.ShapeDtypeStruct((nq, cands), F32),
        in_specs=[hbm, hbm, hbm, vmem, vmem],
        out_specs=vmem,
        scratch_shapes=[
            pltpu.VMEM((ndocs, slots, dim), BF16),
            pltpu.VMEM((rows, width), BF16),
            pltpu.VMEM((width, dim), BF16),
            pltpu.VMEM((nt, rows, dim), BF16),
            pltpu.VMEM((no, 2, rows * nt // 2, dim), BF16),
            pltpu.VMEM((no, 1, cap), I32),
            pltpu.VMEM((no, 1, cap), I32),
            pltpu.SMEM((no, 1, cap), I32),
            pltpu.VMEM((2 * no, 1, cap * slots), F32),
            pltpu.VMEM((no, cap), I32),
            pltpu.VMEM((nq, no, cands), BF16),
            pltpu.VMEM((nq, 1, cands), F32),
            pltpu.VMEM((no, per * nt, cap), F32),
            pltpu.VMEM((no // nt, nt, per * nt, cap), F32),
            pltpu.VMEM((no // nt, 1, cap), F32),
            pltpu.VMEM((no, 1, cap), F32),
            pltpu.VMEM((no, cap), F32),
            dma((3,)),
            dma((nt,)),
            dma((nt,)),
            dma((no,)),
            dma((no,)),
            dma((no, 2)),
            dma((ny,)),
            dma((no,)),
            dma((no,)),
            dma((no,)),
            dma((no,)),
            dma((no // nt, nt)),
            dma((no // nt, nt)),
            dma((no,)),
            dma,
        ],
        compiler_params=pltpu.CompilerParams(
            collective_id=0, has_side_effects=True, vmem_limit_bytes=48 * 2**20
        ),
    )(
        doc_vectors,
        query_states.reshape(rows, width),
        proj_weight,
        document_token_length.reshape(-1, min(128, ndocs)),
        candidates,
    )


def solution(mesh, ny=4):
    no, nt = mesh.shape["doc"], mesh.shape["tok"]
    placed = (P("doc", "tok", None), P(), P("doc", "tok", None), P("doc"), P("doc", None))
    return jax.shard_map(
        functools.partial(on_device, ny, no // ny, nt),
        mesh=mesh, in_specs=placed, out_specs=P("doc", None), check_vma=False,
    )
```

```python
import functools

import jax
import jax.numpy as jnp
from jax import lax
from jax.experimental import pallas as pl
from jax.experimental.pallas import tpu as pltpu
from jax.sharding import PartitionSpec as P

MESH = pl.DeviceIdType.MESH
F32, BF16, I32 = jnp.float32, jnp.bfloat16, jnp.int32
NT = (((1,), (1,)), ((), ()))
GROUP = 4
WAVES = ((3, 4), (5, 6), (), (7,))
LAG = 4


def iota(shape, dim):
    return lax.broadcasted_iota(I32, shape, dim)


def schedule(ny, nz):
    half = nz // 2
    steps = [0.0] + [1.9 + 1.1 * ((k + 1) // 2) for k in range(1, nz)]
    steps[nz - 1] += 1.0 if half > 2 else 0.0
    entries = [(steps[k] + (3.4 if p else 0.0), p, k) for k in range(nz) for p in range(ny)]
    return [(k, p) for _, p, k in sorted(entries, key=lambda e: (e[0], e[2], e[1]))]


def kernel(
    ny, nz, nt, docs_hbm, qs_hbm, w_hbm, len_hbm, cand_hbm, out_ref,
    docs, qs, qrow, w, len_ref, cand_ref, ublk, qall, lists_out, lists_z, lists_in, lists, combs, onehots, ranks,
    raw, best, inbox, sums, table, table2,
    in_sem, a_send, a_recv, z_send, y_send, sib_send, q_recv, l_send, l_recv, yl_send, yl_recv,
    m_send, m_recv, t_send, t_recv, s_sem,
):
    no = ny * nz
    d, t = lax.axis_index("doc"), lax.axis_index("tok")
    y, z, c = d // nz, d % nz, t % 2
    sibling = t + 1 - 2 * c
    nq, cands = cand_ref.shape
    ndocs = docs.shape[0]
    slots = docs.shape[1]
    shift = ndocs.bit_length() - 1
    per = qs.shape[1]
    qrows = nq * per * nt
    per_query = per * nt
    cap = lists_in.shape[2]
    order = schedule(ny, nz)
    groups = no // GROUP

    pairs = ((qs_hbm, qs), (w_hbm, w), (cand_hbm, cand_ref), (len_hbm, len_ref), (docs_hbm, docs))
    loads = [pltpu.make_async_copy(src, dst, in_sem.at[i]) for i, (src, dst) in enumerate(pairs)]
    for load in loads:
        load.start()

    barrier = pltpu.get_barrier_semaphore()

    def greet(doc, tok):
        pl.semaphore_signal(barrier, inc=1, device_id={"doc": doc, "tok": tok}, device_id_type=MESH)

    for p in range(1, nz):
        greet(y * nz + (z + p) % nz, t)
    for p in range(1, ny):
        greet(((y + p) % ny) * nz + z, t)
    for p in range(1, nt):
        greet(d, (t + p) % nt)

    def send(src, dst, ssem, rsem, doc, tok):
        return pltpu.make_async_remote_copy(
            src_ref=src, dst_ref=dst, send_sem=ssem, recv_sem=rsem,
            device_id={"doc": doc, "tok": tok}, device_id_type=MESH,
        )

    def loop(first, last, do):
        def body(i, carry):
            do(i)
            return carry

        lax.fori_loop(first, last, body, 0)

    loads[0].wait()
    for q in range(nq):
        qrow[per * q : per * (q + 1)] = qs[q].astype(F32)
    loads[1].wait()
    proj = jnp.dot(qrow[...].astype(BF16), w[...], preferred_element_type=F32)
    unit = proj * lax.rsqrt(jnp.sum(proj * proj, axis=-1, keepdims=True) + 1e-06)
    ublk[t] = unit.astype(BF16)

    pl.semaphore_wait(barrier, nt - 1 + nz - 1 + ny - 1)

    def send_unit(p):
        return send(ublk.at[t], ublk.at[t], a_send.at[p], a_recv.at[t], d, (t + p) % nt)

    for p in range(1, nt):
        send_unit(p).start()

    loads[2].wait()
    cand = cand_ref[...]
    shard_rows = []
    for q in range(nq):
        shard_rows.append((iota((no, cands), 0) == (cand[q : q + 1] >> shift)).astype(F32))
    before = (iota((cands, cands), 0) < iota((cands, cands), 1)).astype(BF16)
    prefix = jnp.dot(
        jnp.concatenate(shard_rows, axis=0).astype(BF16), before, preferred_element_type=F32
    )
    base = jnp.zeros((no, 1), F32)
    coded = jnp.zeros((2 * no, cap), F32)
    for q in range(nq):
        mine = shard_rows[q]
        rank = jnp.sum(mine * (prefix[no * q : no * (q + 1)] + base), axis=0, keepdims=True)
        base = base + jnp.sum(mine, axis=1, keepdims=True)
        ranks[q] = rank
        onehots[q] = mine.astype(BF16)
        local = cand[q : q + 1] & (ndocs - 1)
        high = (local >> 8) + (ndocs >> 8) * q
        low = local & 255
        rank_rows = (iota((cap, cands), 0).astype(F32) == rank).astype(BF16)
        lhs = jnp.concatenate([mine * high.astype(F32), mine * low.astype(F32)], axis=0)
        coded = coded + lax.dot_general(lhs.astype(BF16), rank_rows, NT, preferred_element_type=F32)
    packed = coded[:no].astype(I32) * 256 + coded[no:].astype(I32)
    for s in range(no):
        lists_out[s % nz, s // nz] = packed[s : s + 1]
    lists_z[z] = lists_out[z]

    def offset(k):
        return jnp.where(k % 2 == 1, (k + 1) // 2, -(k // 2))

    def send_list(k):
        to = (z + nz + offset(k)) % nz
        return send(lists_out.at[to], lists_z.at[z], l_send.at[k], l_recv.at[z], y * nz + to, t)

    loop(1, nz, lambda k: send_list(k).start())

    row, col = iota((qrows, qrows), 0), iota((qrows, qrows), 1)
    from_row = ((row // per) % nt) * (per * nq) + (row // per_query) * per + row % per
    sorting = (from_row == col).astype(BF16)

    def unit_arrived(p):
        src = (t + p) % nt
        send(ublk.at[src], ublk.at[src], a_send.at[0], a_recv.at[src], d, src).wait_recv()

    loop(1, nt, unit_arrived)
    mixed = jnp.concatenate([ublk[i] for i in range(nt)], axis=0)
    sorted_rows = jnp.dot(sorting, mixed, preferred_element_type=F32).astype(BF16)
    half = qrows // 2
    qall[d, 0] = sorted_rows[:half]
    qall[d, 1] = sorted_rows[half:]

    def send_z(k):
        to = (z + nz + offset(k)) % nz
        return send(qall.at[d, c], qall.at[d, c], z_send.at[k], q_recv.at[d, c], y * nz + to, t)

    loop(1, nz, lambda k: send_z(k).start())

    def owner(k, p):
        return ((y + p) % ny) * nz + (z + nz + offset(k)) % nz

    def send_y(k, p):
        o = owner(k, 0)
        return send(qall.at[o, c], qall.at[o, c], y_send.at[k, p], q_recv.at[o, c], ((y + p) % ny) * nz + z, t)

    def send_row(k, p):
        o, to = owner(k, 0), (y + p) % ny
        return send(lists_z.at[o % nz, to], lists_in.at[o], yl_send.at[k, p], yl_recv.at[o], to * nz + z, t)

    def share(o):
        return send(qall.at[o, c], qall.at[o, c], sib_send.at[o], q_recv.at[o, c], d, sibling)

    def forward(k, own=False):
        o = owner(k, 0)
        if not own:
            share(o).wait_recv()
        for p in range(1, ny):
            send_y(k, p).start()
        if not own:
            share(o).start()
            send(lists_z.at[o % nz], lists_z.at[o % nz], l_send.at[0], l_recv.at[o % nz], o, t).wait_recv()
        for p in range(1, ny):
            send_row(k, p).start()
        lists_in[o] = lists_z[o % nz, y]

    def to_smem(o):
        return pltpu.make_async_copy(lists_in.at[o], lists.at[o], s_sem.at[o])

    def entry(g, i):
        k, p = jnp.int32(0), jnp.int32(0)
        for n in range(groups):
            k = jnp.where(g == n, order[GROUP * n + i][0], k)
            p = jnp.where(g == n, order[GROUP * n + i][1], p)
        return k, p, owner(k, p)

    def receive(g):
        for i in range(GROUP):
            k, p, o = entry(g, i)

            @pl.when(p != 0)
            def _():
                share(o).wait_recv()
                share(o).start()
                send(lists_in.at[o], lists_in.at[o], l_send.at[0], yl_recv.at[o], o, t).wait_recv()

            to_smem(o).start()

    def complete(g):
        for i in range(GROUP):
            k, p, o = entry(g, i)

            @pl.when(o != d)
            def _():
                other = qall.at[o, 1 - c]
                send(other, other, sib_send.at[o], q_recv.at[o, 1 - c], d, sibling).wait_recv()

            to_smem(o).wait()

    lane = iota((8, cap), 1)
    lanes = len_ref.shape[1]
    position = t * slots + lane % slots
    blocks = cap // slots

    def combine(o):
        line = jnp.broadcast_to(lists_in[o], (8, cap))
        doc_id = line & (ndocs - 1)
        length = jnp.zeros((8, cap), I32)
        for r in range(len_ref.shape[0]):
            found = jnp.take_along_axis(
                jnp.broadcast_to(len_ref[r : r + 1], (8, lanes)), doc_id % lanes, axis=1
            )
            length = jnp.where(doc_id // lanes == r, found, length)
        combs[o] = (line >> shift) * 256 + length

    def merge(a, b, dist):
        keep = ((lane // dist) % 2 == 0)[None]
        a_back = pltpu.roll(a, cap - dist, 2)
        b_on = pltpu.roll(b, dist, 2)
        return jnp.maximum(jnp.where(keep, a, b_on), jnp.where(keep, a_back, b))

    def tile(o, query, comb, v):
        both = (v, v + slots // 2)
        parts = []
        for u in both:
            for n in range(blocks):
                parts.append(docs[lists[o, 0, n * slots + u] & (ndocs - 1)])
        sims = lax.dot_general(query, jnp.concatenate(parts, axis=0), NT, preferred_element_type=F32)
        out = []
        for h, u in enumerate(both):
            block = sims[:, h * cap : (h + 1) * cap].reshape(nq, per_query // 8, 8, cap)
            here = jnp.take_along_axis(comb, (lane // slots) * slots + u, axis=1)
            whose, until = here >> 8, here & 255
            picked = block[0]
            for q in range(1, nq):
                picked = jnp.where((whose == q)[None], block[q], picked)
            out.append(jnp.where((position < until)[None], picked, F32(-1e30)))
        return out

    def fold(leaf, v, dist):
        if dist == slots // 2:
            return merge(*leaf(v), dist)
        return merge(fold(leaf, v, dist * 2), fold(leaf, v + dist, dist * 2), dist)

    def put(j, value):
        best[j + 1] = value.reshape(per_query, cap)

    def kept(v):
        return raw[v], raw[v + slots // 2]

    def compute(g):
        put(GROUP * g - 1, fold(kept, 0, 1))
        for i in range(GROUP):
            o = entry(g, i)[2]
            query = jnp.concatenate([qall[o, 0], qall[o, 1]], axis=0)
            comb = combs[o]
            leaf = functools.partial(tile, o, query, comb)
            if i < GROUP - 1:
                put(GROUP * g + i, fold(leaf, 0, 1))
            else:
                for v in range(slots // 2):
                    raw[v], raw[v + slots // 2] = leaf(v)
        for i in range(GROUP):
            combine(entry(jnp.minimum(g + 1, groups - 1), i)[2])

    def send_best(j):
        return send(best.at[j + 1], inbox.at[j // nt, t], m_send.at[j], m_recv.at[j // nt, t], d, j % nt)

    def give_best(j):
        @pl.when((j >= 0) & (j % nt != t))
        def _():
            send_best(j).start()

    def target(m):
        j = t + nt * m
        o = jnp.int32(0)
        for i in range(GROUP):
            o = jnp.where(j % GROUP == i, entry(j // GROUP, i)[2], o)
        return o

    def send_sum(m, tp, o):
        return (o == d) & (tp == t), send(sums.at[m], table.at[d], t_send.at[m, tp], t_recv.at[d], o, tp)

    def reduce(m):
        total = best[t + nt * m + 1]

        def more(p, total):
            src = (t + p) % nt
            send(inbox.at[m, src], inbox.at[m, src], m_send.at[0], m_recv.at[m, src], d, src).wait_recv()
            return jnp.maximum(total, inbox[m, src])

        total = lax.fori_loop(1, nt, more, total)
        sums[m] = jnp.sum(total, axis=0, keepdims=True)
        o = target(m)

        def give(tp):
            mine, copy = send_sum(m, tp, o)

            @pl.when(mine)
            def _():
                table[d] = sums[m]

            @pl.when(jnp.logical_not(mine))
            def _():
                copy.start()

        loop(0, nt, give)

    forward(0, own=True)
    loop(1, min(3, nz), forward)
    receive(0)
    loads[3].wait()
    for i in range(GROUP):
        combine(entry(0, i)[2])
    loads[4].wait()

    passing = {n: [k for k in WAVES[n] if k < nz] for n in range(min(groups, len(WAVES)))}
    summing = [(nt * (m + 1) - 1) // GROUP + LAG for m in range(no // nt)]

    def step(g):
        for n, ks in passing.items():
            if ks:

                @pl.when(g == n)
                def _():
                    loop(ks[0], ks[-1] + 1, forward)

        @pl.when(g < groups - 1)
        def _():
            receive(g + 1)

        complete(g)
        compute(g)
        for i in range(GROUP):
            give_best(GROUP * g + i - 1)
        for m, n in enumerate(summing):
            if n < groups:
                pl.when(g == n)(functools.partial(reduce, m))

    loop(0, groups, step)
    put(no - 1, fold(kept, 0, 1))
    give_best(jnp.int32(no - 1))
    for m, n in enumerate(summing):
        if n >= groups:
            reduce(m)

    def drained_units(p):
        send_unit(p).wait_send()

    def drained_z(k):
        send_z(k).wait_send()
        send_list(k).wait_send()

    def drained_y(k):
        for p in range(1, ny):
            send_y(k, p).wait_send()
            send_row(k, p).wait_send()

    def drained_owner(o):
        @pl.when(o != d)
        def _():
            share(o).wait_send()

        @pl.when(o % nt != t)
        def _():
            send_best(o).wait_send()

    loop(1, nt, drained_units)
    loop(1, nz, drained_z)
    loop(0, nz, drained_y)
    loop(0, no, drained_owner)

    def score_arrived(s):
        @pl.when(jnp.logical_not((s == d) & (t == order.index((0, 0)) % nt)))
        def _():
            send(table.at[s], table.at[s], t_send.at[0, 0], t_recv.at[s], s, t).wait_recv()

    loop(0, no, score_arrived)

    for s in range(no):
        table2[s : s + 1] = table[s]
    whole = table2[...]
    top = whole.astype(BF16).astype(F32)
    rest = whole - top
    middle = rest.astype(BF16).astype(F32)
    stacked = [top, middle, rest - middle]
    pad = 128 - 3 * no
    stacked.append(jnp.zeros((pad, cap), F32))
    turned = jnp.transpose(jnp.concatenate(stacked, axis=0)).astype(BF16)
    for q in range(nq):
        mine = onehots[q]
        select = jnp.concatenate([mine, mine, mine, jnp.zeros((pad, cands), BF16)], axis=0)
        found = jnp.dot(turned, select, preferred_element_type=F32)
        hit = iota((cap, cands), 0).astype(F32) == ranks[q]
        out_ref[q : q + 1] = jnp.sum(jnp.where(hit, found, F32(0.0)), axis=0, keepdims=True)

    def sums_left(i):
        mine, copy = send_sum(i // nt, i % nt, target(i // nt))

        @pl.when(jnp.logical_not(mine))
        def _():
            copy.wait_send()

    loop(0, no, sums_left)


def on_device(ny, nz, nt, query_states, proj_weight, doc_vectors, document_token_length, candidates):
    nq, per, width = query_states.shape
    ndocs, slots, dim = doc_vectors.shape
    cands = candidates.shape[1]
    no = ny * nz
    cap = 2 * nq * cands // no
    rows = nq * per
    lanes = min(128, ndocs)
    dma = pltpu.SemaphoreType.DMA
    hbm = pl.BlockSpec(memory_space=pl.ANY)
    return pl.pallas_call(
        functools.partial(kernel, ny, nz, nt),
        out_shape=jax.ShapeDtypeStruct((nq, cands), F32),
        in_specs=[hbm] * 5,
        out_specs=pl.BlockSpec(memory_space=pltpu.VMEM),
        scratch_shapes=[
            pltpu.VMEM((ndocs, slots, dim), BF16),
            pltpu.VMEM((nq, per, width), BF16),
            pltpu.VMEM((rows, width), F32),
            pltpu.VMEM((width, dim), BF16),
            pltpu.VMEM((ndocs // lanes, lanes), I32),
            pltpu.VMEM((nq, cands), I32),
            pltpu.VMEM((nt, rows, dim), BF16),
            pltpu.VMEM((no, 2, rows * nt // 2, dim), BF16),
            pltpu.VMEM((nz, ny, 1, cap), I32),
            pltpu.VMEM((nz, ny, 1, cap), I32),
            pltpu.VMEM((no, 1, cap), I32),
            pltpu.SMEM((no, 1, cap), I32),
            pltpu.VMEM((no, 8, cap), I32),
            pltpu.VMEM((nq, no, cands), BF16),
            pltpu.VMEM((nq, 1, cands), F32),
            pltpu.VMEM((slots, per * nt // 8, 8, cap), F32),
            pltpu.VMEM((no + 1, per * nt, cap), F32),
            pltpu.VMEM((no // nt, nt, per * nt, cap), F32),
            pltpu.VMEM((no // nt, 1, cap), F32),
            pltpu.VMEM((no, 1, cap), F32),
            pltpu.VMEM((no, cap), F32),
            dma((5,)),
            dma((nt,)),
            dma((nt,)),
            dma((nz,)),
            dma((nz, ny)),
            dma((no,)),
            dma((no, 2)),
            dma((nz,)),
            dma((nz,)),
            dma((nz, ny)),
            dma((no,)),
            dma((no,)),
            dma((no // nt, nt)),
            dma((no // nt, nt)),
            dma((no,)),
            dma((no,)),
        ],
        compiler_params=pltpu.CompilerParams(
            collective_id=0, has_side_effects=True, vmem_limit_bytes=60 * 2**20
        ),
    )(
        doc_vectors,
        query_states,
        proj_weight,
        document_token_length.reshape(-1, lanes),
        candidates,
    )


def solution(mesh, ny=4):
    no, nt = mesh.shape["doc"], mesh.shape["tok"]
    placed = (P("doc", "tok", None), P(), P("doc", "tok", None), P("doc"), P("doc", None))
    return jax.shard_map(
        functools.partial(on_device, ny, no // ny, nt),
        mesh=mesh, in_specs=placed, out_specs=P("doc", None), check_vma=False,
    )
```

```python
import functools

import jax
import jax.numpy as jnp
from jax import lax
from jax.experimental import pallas as pl
from jax.experimental.pallas import tpu as pltpu
from jax.sharding import PartitionSpec as P

MESH = pl.DeviceIdType.MESH
F32, BF16, I32 = jnp.float32, jnp.bfloat16, jnp.int32
NT = (((1,), (1,)), ((), ()))
GROUP = 2
LAG = 4


def iota(shape, dim):
    return lax.broadcasted_iota(I32, shape, dim)


def along(k):
    return (k + 1) // 2 if k % 2 else -(k // 2)


def schedule(ny, nz):
    near = [5.0 + 1.0 * m for m in range(nz // 2)]
    entries = [(near[m] + (3.0 if p else 0.0), m, p) for m in range(nz // 2) for p in range(ny)]
    return [(m, p) for _, m, p in sorted(entries)]


def kernel(
    ny, nz, nt, docs_hbm, qs_hbm, w_hbm, len_hbm, cand_hbm, out_ref,
    docs, docs2, qs, qrow, w, len_ref, cand_ref, ublk, pieces, qall, sorting, lists_out, lists_z, lists_in, lists, combs, onehots, ranks,
    sorted_q, raw, best, inbox, sums, table, table2,
    in_sem, a_send, a_recv, b_send, b_recv, v_send, v_recv, z_send, z_recv, y_send, d_send, d_recv, q_recv, l_send, l_recv, yl_send, yl_recv,
    m_send, m_recv, t_send, t_recv, s_sem,
):
    no = ny * nz
    d, t = lax.axis_index("doc"), lax.axis_index("tok")
    y, z, c = d // nz, d % nz, t % 2
    sibling = t + 1 - 2 * c
    nq, cands = cand_ref.shape
    ndocs = docs.shape[0]
    slots = docs.shape[1]
    shift = ndocs.bit_length() - 1
    per = qs.shape[1]
    qrows = nq * per * nt
    per_query = per * nt
    cap = lists_in.shape[2]
    order = schedule(ny, nz)
    groups = no // 2 // GROUP
    nx = nt // 2
    x, odd = t // 2, (z + c) % 2
    places = [[k for k in range(nz) if along(k) % 2 == side] for side in (0, 1)]

    pairs = ((qs_hbm, qs), (w_hbm, w), (cand_hbm, cand_ref), (len_hbm, len_ref), (docs_hbm, docs))
    loads = [pltpu.make_async_copy(src, dst, in_sem.at[i]) for i, (src, dst) in enumerate(pairs)]
    for load in loads:
        load.start()

    barrier = pltpu.get_barrier_semaphore()

    def greet(doc, tok):
        pl.semaphore_signal(barrier, inc=1, device_id={"doc": doc, "tok": tok}, device_id_type=MESH)

    for p in range(1, nz):
        greet(y * nz + (z + p) % nz, t)
    for p in range(1, ny):
        greet(((y + p) % ny) * nz + z, t)
    for p in range(1, nt):
        greet(d, (t + p) % nt)

    def send(src, dst, ssem, rsem, doc, tok):
        return pltpu.make_async_remote_copy(
            src_ref=src, dst_ref=dst, send_sem=ssem, recv_sem=rsem,
            device_id={"doc": doc, "tok": tok}, device_id_type=MESH,
        )

    def loop(first, last, do):
        def body(i, carry):
            do(i)
            return carry

        lax.fori_loop(first, last, body, 0)

    loads[0].wait()
    for q in range(nq):
        qrow[per * q : per * (q + 1)] = qs[q].astype(F32)
    loads[1].wait()
    proj = jnp.dot(qrow[...].astype(BF16), w[...], preferred_element_type=F32)
    unit = proj * lax.rsqrt(jnp.sum(proj * proj, axis=-1, keepdims=True) + 1e-06)
    ublk[0] = unit.astype(BF16)

    pl.semaphore_wait(barrier, nt - 1 + nz - 1 + ny - 1)

    def offset(k):
        return jnp.where(k % 2 == 1, (k + 1) // 2, -(k // 2))

    def send_z(k):
        to = (z + nz - offset(k)) % nz
        return send(ublk.at[0], ublk.at[k], z_send.at[k], z_recv.at[k], y * nz + to, t)

    def core_of(k):
        return (z + along(k) % 2) % 2

    def rank_of(k):
        return places[along(k) % 2].index(k)

    def to_core(k, p):
        return (x + p) % nx * 2 + core_of(k)

    def send_tok(k, p):
        return send(ublk.at[k], qall.at[rank_of(k), 0, t], a_send.at[k, p], a_recv.at[k, t], d, to_core(k, p))

    def rest(k):
        return qall.at[rank_of(k), pl.ds(1, ny - 1), t]

    def send_rest(k, p):
        return send(
            pieces.at[rank_of(k), pl.ds(1, ny - 1)], rest(k), b_send.at[k, p], b_recv.at[k, t], d, to_core(k, p)
        )

    def send_piece(k, p):
        return send(
            ublk.at[k], pieces.at[rank_of(k), ny - p], v_send.at[k, p], v_recv.at[k, ny - p],
            ((y + p) % ny) * nz + z, t,
        )

    def each_tok(k, make, do):
        pl.when(core_of(k) != c)(lambda: do(make(k, 0)))
        for p in range(1, nx):
            do(make(k, p))

    def go(copy):
        copy.start()

    def left(copy):
        copy.wait_send()

    for k in range(1, nz):
        send_z(k).start()
    def spread(k):
        each_tok(k, send_tok, go)
        if along(k) % 2:
            for p in range(1, ny):
                send_piece(k, p).start()

        @pl.when(core_of(k) == c)
        def _():
            qall[rank_of(k), 0, t] = ublk[k]

    spread(0)

    loads[2].wait()
    cand = cand_ref[...]
    shard_rows = []
    for q in range(nq):
        shard_rows.append((iota((no, cands), 0) == (cand[q : q + 1] >> shift)).astype(F32))
    before = (iota((cands, cands), 0) < iota((cands, cands), 1)).astype(BF16)
    prefix = jnp.dot(
        jnp.concatenate(shard_rows, axis=0).astype(BF16), before, preferred_element_type=F32
    )
    base = jnp.zeros((no, 1), F32)
    coded = jnp.zeros((2 * no, cap), F32)
    for q in range(nq):
        mine = shard_rows[q]
        rank = jnp.sum(mine * (prefix[no * q : no * (q + 1)] + base), axis=0, keepdims=True)
        base = base + jnp.sum(mine, axis=1, keepdims=True)
        number = rank.astype(I32)
        ranks[q] = (number % (cap // slots)) * slots + number // (cap // slots)
        onehots[q] = mine.astype(BF16)
        local = cand[q : q + 1] & (ndocs - 1)
        high = (local >> 8) + (ndocs >> 8) * q
        low = local & 255
        rank_rows = (iota((cap, cands), 0).astype(F32) == rank).astype(BF16)
        lhs = jnp.concatenate([mine * high.astype(F32), mine * low.astype(F32)], axis=0)
        coded = coded + lax.dot_general(lhs.astype(BF16), rank_rows, NT, preferred_element_type=F32)
    packed = coded[:no].astype(I32) * 256 + coded[no:].astype(I32)
    packed = jnp.where(iota((no, cap), 1).astype(F32) < base, packed, (nq - 1) * ndocs)
    for s in range(no):
        lists_out[s % nz, s // nz] = packed[s : s + 1]
    lists_z[z] = lists_out[z]

    def send_list(k):
        to = (z + nz + offset(k)) % nz
        return send(lists_out.at[to], lists_z.at[z], l_send.at[k], l_recv.at[z], y * nz + to, t)

    pl.when(c == z % 2)(lambda: loop(1, nz, lambda k: send_list(k).start()))

    row, col = iota((qrows, qrows), 0), iota((qrows, qrows), 1)
    from_row = ((row // per) % nt) * (per * nq) + (row // per_query) * per + row % per
    sorting[...] = (from_row == col).astype(BF16)

    def relay(k):
        send_z(k).wait_recv()
        spread(k)

    def relay_rest(k):
        for p in range(1, ny):
            send_piece(k, ny - p).wait_recv()
        each_tok(k, send_rest, go)

        @pl.when(core_of(k) == c)
        def _():
            for p in range(1, ny):
                qall[rank_of(k), p, t] = pieces[rank_of(k), p]

    def owner(k, p):
        return ((y + p) % ny) * nz + (z + nz + offset(k)) % nz

    def send_y(m, p):
        return send(
            qall.at[m, 0], qall.at[m, ny - p], y_send.at[m, p], q_recv.at[m, ny - p], ((y + p) % ny) * nz + z, t
        )

    def send_row(m, p):
        o, to = owner(place(m), 0), (y + p) % ny
        slot = m * ny + ny - p
        return send(
            lists_z.at[o % nz, to], lists_in.at[slot], yl_send.at[m, p], yl_recv.at[slot], to * nz + z, t
        )

    def place(m):
        return jnp.where(odd == 0, places[0][m], places[1][m])

    def gathered(k, arrivals):
        for p in range(1, nt):
            src = (t + p) % nt
            send(ublk.at[0], ublk.at[0], d_send, arrivals.at[k, src], d, sibling).wait_recv()

    def gathered_rest(k):
        for p in range(1, nt):
            src = (t + p) % nt
            part = pieces.at[0, pl.ds(1, ny - 1)]
            send(part, part, d_send, b_recv.at[k, src], d, sibling).wait_recv()

    def forward(m):
        @pl.when(odd == 0)
        def _():
            gathered(places[0][m], a_recv)
            for p in range(1, ny):
                send_y(m, p).start()

    def forward_list(m):
        k = place(m)
        o = owner(k, 0)

        @pl.when(k != 0)
        def _():
            send(lists_z.at[o % nz], lists_z.at[o % nz], l_send.at[0], l_recv.at[o % nz], d, sibling).wait_recv()

        for p in range(1, ny):
            send_row(m, p).start()
        lists_in[m * ny] = lists_z[o % nz, y]

    def row_arrived(m, p):
        slot = m * ny + p
        send(lists_in.at[slot], lists_in.at[slot], d_send, yl_recv.at[slot], d, sibling).wait_recv()

    def entry(g, i):
        m, k, p = jnp.int32(0), jnp.int32(0), jnp.int32(0)
        for n in range(groups):
            step_m, step_p = order[GROUP * n + i]
            m = jnp.where(g == n, step_m, m)
            k = jnp.where(g == n, place(step_m), k)
            p = jnp.where(g == n, step_p, p)
        return m, k, p, owner(k, p), m * ny + p

    def complete(g):
        for i in range(GROUP):
            m, k, p, _, _ = entry(g, i)

            @pl.when((odd == 0) & (p != 0))
            def _():
                send(qall.at[m, p], qall.at[m, p], d_send, q_recv.at[m, p], d, sibling).wait_recv()

            @pl.when((odd == 1) & (p == 0))
            def _():
                gathered(k, a_recv)

            @pl.when((odd == 1) & (p == 1))
            def _():
                gathered_rest(k)

    lane = iota((8, cap), 1)
    lanes = len_ref.shape[1]
    position = t * slots + lane % slots
    position2 = sibling * slots + lane % slots
    blocks = cap // slots

    def combine(slot):
        line = jnp.broadcast_to(lists_in[slot], (8, cap))
        doc_id = line & (ndocs - 1)
        length = jnp.zeros((8, cap), I32)
        for r in range(len_ref.shape[0]):
            found = jnp.take_along_axis(
                jnp.broadcast_to(len_ref[r : r + 1], (8, lanes)), doc_id % lanes, axis=1
            )
            length = jnp.where(doc_id // lanes == r, found, length)
        combs[slot] = (line >> shift) * 256 + length

    def merge(a, b, dist):
        keep = ((lane // dist) % 2 == 0)[None]
        a_back = pltpu.roll(a, cap - dist, 2)
        b_on = pltpu.roll(b, dist, 2)
        return jnp.maximum(jnp.where(keep, a, b_on), jnp.where(keep, a_back, b))

    window = nq // 2

    def starts(o):
        first, extra = [], jnp.int32(0)
        for v in range(blocks):
            first.append(jnp.minimum((lists[o, 0, slots * v] >> shift) & (nq - 1), nq - window))
            last = (lists[o, 0, slots * v + slots - 1] >> shift) & (nq - 1)
            extra = extra + jnp.where(last - first[v] >= window, v, 0)
        return first, extra & (blocks - 1)

    def product(o, query, v):
        picks = [lists[o, 0, slots * v + n] & (ndocs - 1) for n in range(slots)]
        out = []
        for source in (docs, docs2):
            matrix = jnp.concatenate([source[i] for i in picks], axis=0)
            out.append(lax.dot_general(query, matrix, NT, preferred_element_type=F32))
        return out

    def chosen(sims, h, whose, start, picked):
        block = sims[:, h * cap : (h + 1) * cap].reshape(window, per_query // 8, 8, cap)
        for q in range(window):
            here = block[q] if picked is None else jnp.where((whose == start + q)[None], block[q], picked)
            picked = here
        return picked

    def spread_comb(comb, v, h):
        return jnp.take_along_axis(comb, (2 * v + h) * blocks + lane // slots, axis=1)

    def rows_of(i, start):
        return jnp.concatenate([sorted_q[i, start + q] for q in range(window)], axis=0)

    def further(o, i, comb, extra):
        sims = product(o, rows_of(i, nq - window), extra)
        out = []
        for h in range(2):
            whose = spread_comb(comb, extra, h) >> 8
            out.append([chosen(part, h, whose, nq - window, None) for part in sims])
        return out

    def tile(o, i, comb, first, past, v):
        sims = product(o, rows_of(i, first[v]), v)
        out = []
        for h in range(2):
            here = spread_comb(comb, v, h)
            whose, until = here >> 8, here & 255
            mine = chosen(sims[0], h, whose, first[v], past[h][0])
            theirs = chosen(sims[1], h, whose, first[v], past[h][1])
            mine = jnp.where((position < until)[None], mine, F32(-1e30))
            theirs = jnp.where((position2 < until)[None], theirs, F32(-1e30))
            out.append(jnp.maximum(mine, theirs))
        return out

    def fold(leaf, v, dist):
        if dist == slots:
            return merge(*leaf(v), 1)
        return merge(fold(leaf, v, dist * 2), fold(leaf, v + dist // 2, dist * 2), dist)

    def put(j, value):
        best[j + 1] = value.reshape(per_query, cap)

    def kept(v):
        return raw[2 * v], raw[2 * v + 1]

    def compute(g):
        put(GROUP * g - 1, fold(kept, 0, 2))
        for i in range(GROUP):
            m, _, p, _, _ = entry(g, i)
            mixed = qall[m, p].reshape(qrows, qall.shape[4])
            query = jnp.dot(sorting[...], mixed, preferred_element_type=F32).astype(BF16)
            sorted_q[i] = query.reshape(nq, per_query, query.shape[1])
        for i in range(GROUP):
            o = entry(g, i)[4]
            comb = combs[o]
            first, extra = starts(o)
            leaf = functools.partial(tile, o, i, comb, first, further(o, i, comb, extra))
            if i < GROUP - 1:
                put(GROUP * g + i, fold(leaf, 0, 2))
            else:
                for v in range(blocks):
                    raw[2 * v], raw[2 * v + 1] = leaf(v)
        for i in range(GROUP):
            combine(entry(jnp.minimum(g + 1, groups - 1), i)[4])

    def send_best(j):
        return send(best.at[j + 1], inbox.at[j // nx, x], m_send.at[j], m_recv.at[j // nx, x], d, j % nx * 2 + c)

    def give_best(j):
        @pl.when((j >= 0) & (j % nx != x))
        def _():
            send_best(j).start()

    def target(m):
        j = x + nx * m
        o = jnp.int32(0)
        for i in range(GROUP):
            o = jnp.where(j % GROUP == i, entry(j // GROUP, i)[3], o)
        return o

    def send_sum(m, tp, o):
        return (o == d) & (tp == t), send(sums.at[m], table.at[d], t_send.at[m, tp], t_recv.at[d], o, tp)

    def reduce(m):
        total = best[x + nx * m + 1]
        for p in range(1, nx):
            src = (x + p) % nx
            send(inbox.at[m, src], inbox.at[m, src], d_send, m_recv.at[m, src], d, sibling).wait_recv()
            total = jnp.maximum(total, inbox[m, src])
        sums[m] = jnp.sum(total, axis=0, keepdims=True)
        o = target(m)

        def give(tp):
            mine, copy = send_sum(m, tp, o)

            @pl.when(mine)
            def _():
                table[d] = sums[m]

            @pl.when(jnp.logical_not(mine))
            def _():
                copy.start()

        loop(0, nt, give)

    share_docs = send(docs, docs2, d_send, d_recv, d, sibling)
    loads[3].wait()
    loads[4].wait()
    share_docs.start()
    for k in range(1, nz):
        relay(k)
        if k == 2:
            forward(0)
    for m in range(nz // 2):
        forward_list(m)
    for m in range(1, nz // 2):
        if 2 * m - 1 < len(places[1]):
            relay_rest(places[1][2 * m - 2])
            relay_rest(places[1][2 * m - 1])
        forward(m)
    for m in range(nz // 2):
        for p in range(1, ny):
            row_arrived(m, p)
    to_smem = pltpu.make_async_copy(lists_in, lists, s_sem)
    to_smem.start()
    for i in range(GROUP):
        combine(entry(0, i)[4])
    to_smem.wait()
    share_docs.wait_recv()

    summing = [(nx * (m + 1) - 1) // GROUP + LAG for m in range(no // nt)]

    def step(g):
        complete(g)
        compute(g)
        for i in range(GROUP):
            give_best(GROUP * g + i - 1)
        for m, n in enumerate(summing):
            if n < groups:
                pl.when(g == n)(functools.partial(reduce, m))

    loop(0, groups, step)
    put(no // 2 - 1, fold(kept, 0, 2))
    give_best(jnp.int32(no // 2 - 1))
    for m, n in enumerate(summing):
        if n >= groups:
            reduce(m)

    for k in range(nz):
        each_tok(k, send_tok, left)
        if along(k) % 2:
            each_tok(k, send_rest, left)
            for p in range(1, ny):
                send_piece(k, p).wait_send()
    for k in range(1, nz):
        send_z(k).wait_send()
    for m in range(nz // 2):
        for p in range(1, ny):
            pl.when(odd == 0)(lambda: send_y(m, p).wait_send())
            send_row(m, p).wait_send()
    share_docs.wait_send()
    pl.when(c == z % 2)(lambda: loop(1, nz, lambda k: send_list(k).wait_send()))

    def drained(j):
        @pl.when(j % nx != x)
        def _():
            send_best(j).wait_send()

    loop(0, no // 2, drained)

    def sums_left(i):
        mine, copy = send_sum(i // nt, i % nt, target(i // nt))

        @pl.when(jnp.logical_not(mine))
        def _():
            copy.wait_send()

    loop(0, no, sums_left)

    def score_arrived(s):
        @pl.when(jnp.logical_not((s == d) & (t == order.index((0, 0)) % nx * 2 + z % 2)))
        def _():
            send(table.at[s], table.at[s], t_send.at[0, 0], t_recv.at[s], d, sibling).wait_recv()

    loop(0, no, score_arrived)

    for s in range(no):
        table2[s : s + 1] = table[s]
    whole = table2[...]
    top = whole.astype(BF16).astype(F32)
    rest = whole - top
    middle = rest.astype(BF16).astype(F32)
    stacked = [top, middle, rest - middle]
    pad = 128 - 3 * no
    stacked.append(jnp.zeros((pad, cap), F32))
    turned = jnp.transpose(jnp.concatenate(stacked, axis=0)).astype(BF16)
    for q in range(nq):
        mine = onehots[q]
        select = jnp.concatenate([mine, mine, mine, jnp.zeros((pad, cands), BF16)], axis=0)
        found = jnp.dot(turned, select, preferred_element_type=F32)
        hit = iota((cap, cands), 0) == ranks[q]
        out_ref[q : q + 1] = jnp.sum(jnp.where(hit, found, F32(0.0)), axis=0, keepdims=True)


def on_device(ny, nz, nt, query_states, proj_weight, doc_vectors, document_token_length, candidates):
    nq, per, width = query_states.shape
    ndocs, slots, dim = doc_vectors.shape
    cands = candidates.shape[1]
    no = ny * nz
    cap = 2 * nq * cands // no
    rows = nq * per
    lanes = min(128, ndocs)
    dma = pltpu.SemaphoreType.DMA
    hbm = pl.BlockSpec(memory_space=pl.ANY)
    return pl.pallas_call(
        functools.partial(kernel, ny, nz, nt),
        out_shape=jax.ShapeDtypeStruct((nq, cands), F32),
        in_specs=[hbm] * 5,
        out_specs=pl.BlockSpec(memory_space=pltpu.VMEM),
        scratch_shapes=[
            pltpu.VMEM((ndocs, slots, dim), BF16),
            pltpu.VMEM((ndocs, slots, dim), BF16),
            pltpu.VMEM((nq, per, width), BF16),
            pltpu.VMEM((rows, width), F32),
            pltpu.VMEM((width, dim), BF16),
            pltpu.VMEM((ndocs // lanes, lanes), I32),
            pltpu.VMEM((nq, cands), I32),
            pltpu.VMEM((nz, rows, dim), BF16),
            pltpu.VMEM((nz // 2, ny, rows, dim), BF16),
            pltpu.VMEM((nz // 2, ny, nt, rows, dim), BF16),
            pltpu.VMEM((rows * nt, rows * nt), BF16),
            pltpu.VMEM((nz, ny, 1, cap), I32),
            pltpu.VMEM((nz, ny, 1, cap), I32),
            pltpu.VMEM((no // 2, 1, cap), I32),
            pltpu.SMEM((no // 2, 1, cap), I32),
            pltpu.VMEM((no // 2, 8, cap), I32),
            pltpu.VMEM((nq, no, cands), BF16),
            pltpu.VMEM((nq, 1, cands), I32),
            pltpu.VMEM((GROUP, nq, per * nt, dim), BF16),
            pltpu.VMEM((slots, per * nt // 8, 8, cap), F32),
            pltpu.VMEM((no // 2 + 1, per * nt, cap), F32),
            pltpu.VMEM((no // nt, nt // 2, per * nt, cap), F32),
            pltpu.VMEM((no // nt, 1, cap), F32),
            pltpu.VMEM((no, 1, cap), F32),
            pltpu.VMEM((no, cap), F32),
            dma((5,)),
            dma((nz, nt // 2)),
            dma((nz, nt)),
            dma((nz, nt // 2)),
            dma((nz, nt)),
            dma((nz, ny)),
            dma((nz, ny)),
            dma((nz,)),
            dma((nz,)),
            dma((nz // 2, ny)),
            dma,
            dma,
            dma((nz // 2, ny)),
            dma((nz,)),
            dma((nz,)),
            dma((nz // 2, ny)),
            dma((no // 2,)),
            dma((no // 2,)),
            dma((no // nt, nt // 2)),
            dma((no // nt, nt)),
            dma((no,)),
            dma,
        ],
        compiler_params=pltpu.CompilerParams(
            collective_id=0, has_side_effects=True, vmem_limit_bytes=60 * 2**20
        ),
    )(
        doc_vectors,
        query_states,
        proj_weight,
        document_token_length.reshape(-1, lanes),
        candidates,
    )


def solution(mesh, ny=4):
    no, nt = mesh.shape["doc"], mesh.shape["tok"]
    placed = (P("doc", "tok", None), P(), P("doc", "tok", None), P("doc"), P("doc", None))
    return jax.shard_map(
        functools.partial(on_device, ny, no // ny, nt),
        mesh=mesh, in_specs=placed, out_specs=P("doc", None), check_vma=False,
    )
```

```python
import functools

import jax
import jax.numpy as jnp
from jax import lax
from jax.experimental import pallas as pl
from jax.experimental.pallas import tpu as pltpu
from jax.sharding import PartitionSpec as P

MESH = pl.DeviceIdType.MESH
F32, BF16, I32 = jnp.float32, jnp.bfloat16, jnp.int32
NT = (((1,), (1,)), ((), ()))
GROUP = 2
LAG = 4


def iota(shape, dim):
    return lax.broadcasted_iota(I32, shape, dim)


def along(k):
    return (k + 1) // 2 if k % 2 else -(k // 2)


def schedule(ny, nz):
    own = [(m, 0) for m in range(nz // 2)]
    return own + [(m, p) for m in range(nz // 2) for p in range(1, ny)]


def kernel(
    ny, nz, nt, docs_hbm, qs_hbm, w_hbm, len_hbm, cand_hbm, out_ref,
    docs, docs2, qs, qrow, w, len_ref, cand_ref, ublk, pieces, qall, sorting, lists_out, lists_z, lists_in, near_lists, far_lists, combs, onehots, ranks,
    sorted_q, raw, best, inbox, sums, table, table2,
    in_sem, a_send, a_recv, b_send, b_recv, v_send, v_recv, z_send, z_recv, y_send, d_send, d_recv, q_recv, l_send, l_recv, yl_send, yl_recv,
    m_send, m_recv, t_send, t_recv, s_sem,
):
    no = ny * nz
    d, t = lax.axis_index("doc"), lax.axis_index("tok")
    y, z, c = d // nz, d % nz, t % 2
    sibling = t + 1 - 2 * c
    nq, cands = cand_ref.shape
    ndocs = docs.shape[0]
    slots = docs.shape[1]
    shift = ndocs.bit_length() - 1
    per = qs.shape[1]
    qrows = nq * per * nt
    per_query = per * nt
    cap = lists_in.shape[2]
    order = schedule(ny, nz)
    groups = no // 2 // GROUP
    nx = nt // 2
    depth = nz // 2
    x, odd = t // 2, (z + c) % 2
    places = [[k for k in range(nz) if along(k) % 2 == side] for side in (0, 1)]

    pairs = ((qs_hbm, qs), (w_hbm, w), (cand_hbm, cand_ref), (len_hbm, len_ref), (docs_hbm, docs))
    loads = [pltpu.make_async_copy(src, dst, in_sem.at[i]) for i, (src, dst) in enumerate(pairs)]
    for load in loads:
        load.start()

    barrier = pltpu.get_barrier_semaphore()

    def greet(doc, tok):
        pl.semaphore_signal(barrier, inc=1, device_id={"doc": doc, "tok": tok}, device_id_type=MESH)

    for p in range(1, nz):
        greet(y * nz + (z + p) % nz, t)
    for p in range(1, ny):
        greet(((y + p) % ny) * nz + z, t)
    for p in range(1, nt):
        greet(d, (t + p) % nt)

    def send(src, dst, ssem, rsem, doc, tok):
        return pltpu.make_async_remote_copy(
            src_ref=src, dst_ref=dst, send_sem=ssem, recv_sem=rsem,
            device_id={"doc": doc, "tok": tok}, device_id_type=MESH,
        )

    def loop(first, last, do):
        def body(i, carry):
            do(i)
            return carry

        lax.fori_loop(first, last, body, 0)

    loads[0].wait()
    for q in range(nq):
        qrow[per * q : per * (q + 1)] = qs[q].astype(F32)
    loads[1].wait()
    proj = jnp.dot(qrow[...].astype(BF16), w[...], preferred_element_type=F32)
    unit = proj * lax.rsqrt(jnp.sum(proj * proj, axis=-1, keepdims=True) + 1e-06)
    ublk[0] = unit.astype(BF16)

    pl.semaphore_wait(barrier, nt - 1 + nz - 1 + ny - 1)

    def offset(k):
        return jnp.where(k % 2 == 1, (k + 1) // 2, -(k // 2))

    def send_z(k):
        to = (z + nz - offset(k)) % nz
        return send(ublk.at[0], ublk.at[k], z_send.at[k], z_recv.at[k], y * nz + to, t)

    def core_of(k):
        return (z + along(k) % 2) % 2

    def rank_of(k):
        return places[along(k) % 2].index(k)

    def to_core(k, p):
        return (x + p) % nx * 2 + core_of(k)

    def send_tok(k, p):
        return send(ublk.at[k], qall.at[rank_of(k), 0, t], a_send.at[k, p], a_recv.at[k, t], d, to_core(k, p))

    def rest(k):
        return qall.at[rank_of(k), pl.ds(1, ny - 1), t]

    def send_rest(k, p):
        return send(
            pieces.at[rank_of(k), pl.ds(1, ny - 1)], rest(k), b_send.at[k, p], b_recv.at[k, t], d, to_core(k, p)
        )

    def send_piece(k, p):
        return send(
            ublk.at[k], pieces.at[rank_of(k), ny - p], v_send.at[k, p], v_recv.at[k, ny - p],
            ((y + p) % ny) * nz + z, t,
        )

    def each_tok(k, make, do):
        pl.when(core_of(k) != c)(lambda: do(make(k, 0)))
        for p in range(1, nx):
            do(make(k, p))

    def go(copy):
        copy.start()

    def left(copy):
        copy.wait_send()

    for k in range(1, nz):
        send_z(k).start()
    def spread(k):
        each_tok(k, send_tok, go)
        if along(k) % 2:
            for p in range(1, ny):
                send_piece(k, p).start()

        @pl.when(core_of(k) == c)
        def _():
            qall[rank_of(k), 0, t] = ublk[k]

    spread(0)

    loads[2].wait()
    cand = cand_ref[...]
    shard_rows = []
    for q in range(nq):
        shard_rows.append((iota((no, cands), 0) == (cand[q : q + 1] >> shift)).astype(F32))
    before = (iota((cands, cands), 0) < iota((cands, cands), 1)).astype(BF16)
    prefix = jnp.dot(
        jnp.concatenate(shard_rows, axis=0).astype(BF16), before, preferred_element_type=F32
    )
    base = jnp.zeros((no, 1), F32)
    coded = jnp.zeros((2 * no, cap), F32)
    for q in range(nq):
        mine = shard_rows[q]
        rank = jnp.sum(mine * (prefix[no * q : no * (q + 1)] + base), axis=0, keepdims=True)
        base = base + jnp.sum(mine, axis=1, keepdims=True)
        number = rank.astype(I32)
        ranks[q] = (number % (cap // slots)) * slots + number // (cap // slots)
        onehots[q] = mine.astype(BF16)
        local = cand[q : q + 1] & (ndocs - 1)
        high = (local >> 8) + (ndocs >> 8) * q
        low = local & 255
        rank_rows = (iota((cap, cands), 0).astype(F32) == rank).astype(BF16)
        lhs = jnp.concatenate([mine * high.astype(F32), mine * low.astype(F32)], axis=0)
        coded = coded + lax.dot_general(lhs.astype(BF16), rank_rows, NT, preferred_element_type=F32)
    packed = coded[:no].astype(I32) * 256 + coded[no:].astype(I32)
    packed = jnp.where(iota((no, cap), 1).astype(F32) < base, packed, (nq - 1) * ndocs)
    for s in range(no):
        lists_out[s % nz, s // nz] = packed[s : s + 1]
    lists_z[z] = lists_out[z]

    def send_list(k):
        to = (z + nz + offset(k)) % nz
        return send(lists_out.at[to], lists_z.at[z], l_send.at[k], l_recv.at[z], y * nz + to, t)

    pl.when(c == z % 2)(lambda: loop(1, nz, lambda k: send_list(k).start()))

    row, col = iota((qrows, qrows), 0), iota((qrows, qrows), 1)
    from_row = ((row // per) % nt) * (per * nq) + (row // per_query) * per + row % per
    sorting[...] = (from_row == col).astype(BF16)

    def relay(k):
        send_z(k).wait_recv()
        spread(k)

    def relay_rest(k):
        for p in range(1, ny):
            send_piece(k, ny - p).wait_recv()
        each_tok(k, send_rest, go)

        @pl.when(core_of(k) == c)
        def _():
            for p in range(1, ny):
                qall[rank_of(k), p, t] = pieces[rank_of(k), p]

    def owner(k, p):
        return ((y + p) % ny) * nz + (z + nz + offset(k)) % nz

    def send_y(m, p):
        return send(
            qall.at[m, 0], qall.at[m, ny - p], y_send.at[m, p], q_recv.at[m, ny - p], ((y + p) % ny) * nz + z, t
        )

    def send_row(m, p):
        o, to = owner(place(m), 0), (y + p) % ny
        slot = (ny - p) * depth + m
        return send(
            lists_z.at[o % nz, to], lists_in.at[slot], yl_send.at[m, p], yl_recv.at[slot], to * nz + z, t
        )

    def place(m):
        return jnp.where(odd == 0, places[0][m], places[1][m])

    def gathered(k, arrivals):
        for p in range(1, nt):
            src = (t + p) % nt
            send(ublk.at[0], ublk.at[0], d_send, arrivals.at[k, src], d, sibling).wait_recv()

    def gathered_rest(k):
        for p in range(1, nt):
            src = (t + p) % nt
            part = pieces.at[0, pl.ds(1, ny - 1)]
            send(part, part, d_send, b_recv.at[k, src], d, sibling).wait_recv()

    def forward(m):
        @pl.when(odd == 0)
        def _():
            gathered(places[0][m], a_recv)
            for p in range(1, ny):
                send_y(m, p).start()

    def forward_list(m):
        k = place(m)
        o = owner(k, 0)

        @pl.when(k != 0)
        def _():
            send(lists_z.at[o % nz], lists_z.at[o % nz], l_send.at[0], l_recv.at[o % nz], d, sibling).wait_recv()

        for p in range(1, ny):
            send_row(m, p).start()
        lists_in[m] = lists_z[o % nz, y]

    def row_arrived(m, p):
        slot = p * depth + m
        send(lists_in.at[slot], lists_in.at[slot], d_send, yl_recv.at[slot], d, sibling).wait_recv()

    def entry(g, i):
        m, k, p = jnp.int32(0), jnp.int32(0), jnp.int32(0)
        for n in range(groups):
            step_m, step_p = order[GROUP * n + i]
            m = jnp.where(g == n, step_m, m)
            k = jnp.where(g == n, place(step_m), k)
            p = jnp.where(g == n, step_p, p)
        return m, k, p, owner(k, p), p * depth + m

    def complete(g):
        for i in range(GROUP):
            m, k, p, _, _ = entry(g, i)

            @pl.when((odd == 0) & (p != 0))
            def _():
                send(qall.at[m, p], qall.at[m, p], d_send, q_recv.at[m, p], d, sibling).wait_recv()

            @pl.when((odd == 1) & (p == 0))
            def _():
                gathered(k, a_recv)

            @pl.when((odd == 1) & (p == 1))
            def _():
                gathered_rest(k)

    lane = iota((8, cap), 1)
    lanes = len_ref.shape[1]
    position = t * slots + lane % slots
    position2 = sibling * slots + lane % slots
    blocks = cap // slots

    def combine(slot):
        line = jnp.broadcast_to(lists_in[slot], (8, cap))
        doc_id = line & (ndocs - 1)
        length = jnp.zeros((8, cap), I32)
        for r in range(len_ref.shape[0]):
            found = jnp.take_along_axis(
                jnp.broadcast_to(len_ref[r : r + 1], (8, lanes)), doc_id % lanes, axis=1
            )
            length = jnp.where(doc_id // lanes == r, found, length)
        combs[slot] = (line >> shift) * 256 + length

    def merge(a, b, dist):
        keep = ((lane // dist) % 2 == 0)[None]
        a_back = pltpu.roll(a, cap - dist, 2)
        b_on = pltpu.roll(b, dist, 2)
        return jnp.maximum(jnp.where(keep, a, b_on), jnp.where(keep, a_back, b))

    window = nq // 2

    def starts(lists, o):
        first, extra = [], jnp.int32(0)
        for v in range(blocks):
            first.append(jnp.minimum((lists[o, 0, slots * v] >> shift) & (nq - 1), nq - window))
            last = (lists[o, 0, slots * v + slots - 1] >> shift) & (nq - 1)
            extra = extra + jnp.where(last - first[v] >= window, v, 0)
        return first, extra & (blocks - 1)

    def product(lists, o, query, v):
        picks = [lists[o, 0, slots * v + n] & (ndocs - 1) for n in range(slots)]
        out = []
        for source in (docs, docs2):
            matrix = jnp.concatenate([source[i] for i in picks], axis=0)
            out.append(lax.dot_general(query, matrix, NT, preferred_element_type=F32))
        return out

    def chosen(sims, h, whose, start, picked):
        block = sims[:, h * cap : (h + 1) * cap].reshape(window, per_query // 8, 8, cap)
        for q in range(window):
            here = block[q] if picked is None else jnp.where((whose == start + q)[None], block[q], picked)
            picked = here
        return picked

    def spread_comb(comb, v, h):
        return jnp.take_along_axis(comb, (2 * v + h) * blocks + lane // slots, axis=1)

    def rows_of(i, start):
        return jnp.concatenate([sorted_q[i, start + q] for q in range(window)], axis=0)

    def further(lists, o, i, comb, extra):
        sims = product(lists, o, rows_of(i, nq - window), extra)
        out = []
        for h in range(2):
            whose = spread_comb(comb, extra, h) >> 8
            out.append([chosen(part, h, whose, nq - window, None) for part in sims])
        return out

    def tile(lists, o, i, comb, first, past, v):
        sims = product(lists, o, rows_of(i, first[v]), v)
        out = []
        for h in range(2):
            here = spread_comb(comb, v, h)
            whose, until = here >> 8, here & 255
            mine = chosen(sims[0], h, whose, first[v], past[h][0])
            theirs = chosen(sims[1], h, whose, first[v], past[h][1])
            mine = jnp.where((position < until)[None], mine, F32(-1e30))
            theirs = jnp.where((position2 < until)[None], theirs, F32(-1e30))
            out.append(jnp.maximum(mine, theirs))
        return out

    def fold(leaf, v, dist):
        if dist == slots:
            return merge(*leaf(v), 1)
        return merge(fold(leaf, v, dist * 2), fold(leaf, v + dist // 2, dist * 2), dist)

    def put(j, value):
        best[j + 1] = value.reshape(per_query, cap)

    def kept(v):
        return raw[2 * v], raw[2 * v + 1]

    def compute(g, lists, skipped):
        put(GROUP * g - 1, fold(kept, 0, 2))
        for i in range(GROUP):
            m, _, p, _, _ = entry(g, i)
            mixed = qall[m, p].reshape(qrows, qall.shape[4])
            query = jnp.dot(sorting[...], mixed, preferred_element_type=F32).astype(BF16)
            sorted_q[i] = query.reshape(nq, per_query, query.shape[1])
        for i in range(GROUP):
            slot = entry(g, i)[4]
            comb = combs[slot]
            o = slot - skipped
            first, extra = starts(lists, o)
            past = further(lists, o, i, comb, extra)
            leaf = functools.partial(tile, lists, o, i, comb, first, past)
            if i < GROUP - 1:
                put(GROUP * g + i, fold(leaf, 0, 2))
            else:
                for v in range(blocks):
                    raw[2 * v], raw[2 * v + 1] = leaf(v)
        for i in range(GROUP):
            combine(entry(jnp.minimum(g + 1, groups - 1), i)[4])

    def send_best(j):
        return send(best.at[j + 1], inbox.at[j // nx, x], m_send.at[j], m_recv.at[j // nx, x], d, j % nx * 2 + c)

    def give_best(j):
        @pl.when((j >= 0) & (j % nx != x))
        def _():
            send_best(j).start()

    def target(m):
        j = x + nx * m
        o = jnp.int32(0)
        for i in range(GROUP):
            o = jnp.where(j % GROUP == i, entry(j // GROUP, i)[3], o)
        return o

    def send_sum(m, tp, o):
        return (
            (o == d) & (tp == t),
            send(sums.at[m], table.at[d], t_send.at[m, tp], t_recv, o, tp),
            pltpu.make_async_copy(sums.at[m], table.at[d], t_recv),
        )

    def reduce(m):
        total = best[x + nx * m + 1]
        for p in range(1, nx):
            src = (x + p) % nx
            send(inbox.at[m, src], inbox.at[m, src], d_send, m_recv.at[m, src], d, sibling).wait_recv()
            total = jnp.maximum(total, inbox[m, src])
        sums[m] = jnp.sum(total, axis=0, keepdims=True)
        o = target(m)

        def give(tp):
            mine, copy, keep = send_sum(m, tp, o)

            @pl.when(mine)
            def _():
                keep.start()

            @pl.when(jnp.logical_not(mine))
            def _():
                copy.start()

        loop(0, nt, give)

    share_docs = send(docs, docs2, d_send, d_recv, d, sibling)
    loads[3].wait()
    loads[4].wait()
    share_docs.start()
    for k in range(1, nz):
        relay(k)
        if k == 2:
            forward(0)
    for m in range(nz // 2):
        forward_list(m)
    near_smem = pltpu.make_async_copy(lists_in.at[pl.ds(0, depth)], near_lists, s_sem.at[0])
    far_smem = pltpu.make_async_copy(lists_in.at[pl.ds(depth, no // 2 - depth)], far_lists, s_sem.at[1])
    near_smem.start()
    for i in range(GROUP):
        combine(entry(0, i)[4])

    def step(g, lists, skipped):
        complete(g)
        compute(g, lists, skipped)
        for i in range(GROUP):
            give_best(GROUP * g + i - 1)

    near_groups = depth // GROUP
    for m in range(1, depth):
        if 2 * m - 1 < len(places[1]):
            relay_rest(places[1][2 * m - 2])
            relay_rest(places[1][2 * m - 1])
        forward(m)
        if m == depth - 1:
            for n in range(depth):
                for p in range(1, ny):
                    row_arrived(n, p)
            far_smem.start()
        if m == GROUP - 1:
            near_smem.wait()
            share_docs.wait_recv()
        if (m + 1) % GROUP == 0:
            step(jnp.int32((m + 1) // GROUP - 1), near_lists, 0)
    far_smem.wait()
    summing = [(nx * (m + 1) - 1) // GROUP + LAG for m in range(no // nt)]

    def far_step(g):
        step(g, far_lists, depth)
        for m, n in enumerate(summing):
            if n < groups:
                pl.when(g == n)(functools.partial(reduce, m))

    loop(near_groups, groups, far_step)
    put(no // 2 - 1, fold(kept, 0, 2))
    give_best(jnp.int32(no // 2 - 1))
    for m, n in enumerate(summing):
        if n >= groups:
            reduce(m)

    for k in range(nz):
        each_tok(k, send_tok, left)
        if along(k) % 2:
            each_tok(k, send_rest, left)
            for p in range(1, ny):
                send_piece(k, p).wait_send()
    for k in range(1, nz):
        send_z(k).wait_send()
    for m in range(nz // 2):
        for p in range(1, ny):
            pl.when(odd == 0)(lambda: send_y(m, p).wait_send())
            send_row(m, p).wait_send()
    share_docs.wait_send()
    pl.when(c == z % 2)(lambda: loop(1, nz, lambda k: send_list(k).wait_send()))

    def drained(j):
        @pl.when(j % nx != x)
        def _():
            send_best(j).wait_send()

    loop(0, no // 2, drained)

    def sums_left(i):
        mine, copy, _ = send_sum(i // nt, i % nt, target(i // nt))

        @pl.when(jnp.logical_not(mine))
        def _():
            copy.wait_send()

    loop(0, no, sums_left)

    send(table, table, d_send, t_recv, d, sibling).wait_recv()

    for s in range(no):
        table2[s : s + 1] = table[s]
    whole = table2[...]
    top = whole.astype(BF16).astype(F32)
    rest = whole - top
    middle = rest.astype(BF16).astype(F32)
    stacked = [top, middle, rest - middle]
    pad = 128 - 3 * no
    stacked.append(jnp.zeros((pad, cap), F32))
    turned = jnp.transpose(jnp.concatenate(stacked, axis=0)).astype(BF16)
    for q in range(nq):
        mine = onehots[q]
        select = jnp.concatenate([mine, mine, mine, jnp.zeros((pad, cands), BF16)], axis=0)
        found = jnp.dot(turned, select, preferred_element_type=F32)
        hit = iota((cap, cands), 0) == ranks[q]
        out_ref[q : q + 1] = jnp.sum(jnp.where(hit, found, F32(0.0)), axis=0, keepdims=True)


def on_device(ny, nz, nt, query_states, proj_weight, doc_vectors, document_token_length, candidates):
    nq, per, width = query_states.shape
    ndocs, slots, dim = doc_vectors.shape
    cands = candidates.shape[1]
    no = ny * nz
    cap = 2 * nq * cands // no
    rows = nq * per
    lanes = min(128, ndocs)
    dma = pltpu.SemaphoreType.DMA
    hbm = pl.BlockSpec(memory_space=pl.ANY)
    return pl.pallas_call(
        functools.partial(kernel, ny, nz, nt),
        out_shape=jax.ShapeDtypeStruct((nq, cands), F32),
        in_specs=[hbm] * 5,
        out_specs=pl.BlockSpec(memory_space=pltpu.VMEM),
        scratch_shapes=[
            pltpu.VMEM((ndocs, slots, dim), BF16),
            pltpu.VMEM((ndocs, slots, dim), BF16),
            pltpu.VMEM((nq, per, width), BF16),
            pltpu.VMEM((rows, width), F32),
            pltpu.VMEM((width, dim), BF16),
            pltpu.VMEM((ndocs // lanes, lanes), I32),
            pltpu.VMEM((nq, cands), I32),
            pltpu.VMEM((nz, rows, dim), BF16),
            pltpu.VMEM((nz // 2, ny, rows, dim), BF16),
            pltpu.VMEM((nz // 2, ny, nt, rows, dim), BF16),
            pltpu.VMEM((rows * nt, rows * nt), BF16),
            pltpu.VMEM((nz, ny, 1, cap), I32),
            pltpu.VMEM((nz, ny, 1, cap), I32),
            pltpu.VMEM((no // 2, 1, cap), I32),
            pltpu.SMEM((nz // 2, 1, cap), I32),
            pltpu.SMEM((no // 2 - nz // 2, 1, cap), I32),
            pltpu.VMEM((no // 2, 8, cap), I32),
            pltpu.VMEM((nq, no, cands), BF16),
            pltpu.VMEM((nq, 1, cands), I32),
            pltpu.VMEM((GROUP, nq, per * nt, dim), BF16),
            pltpu.VMEM((slots, per * nt // 8, 8, cap), F32),
            pltpu.VMEM((no // 2 + 1, per * nt, cap), F32),
            pltpu.VMEM((no // nt, nt // 2, per * nt, cap), F32),
            pltpu.VMEM((no // nt, 1, cap), F32),
            pltpu.VMEM((no, 1, cap), F32),
            pltpu.VMEM((no, cap), F32),
            dma((5,)),
            dma((nz, nt // 2)),
            dma((nz, nt)),
            dma((nz, nt // 2)),
            dma((nz, nt)),
            dma((nz, ny)),
            dma((nz, ny)),
            dma((nz,)),
            dma((nz,)),
            dma((nz // 2, ny)),
            dma,
            dma,
            dma((nz // 2, ny)),
            dma((nz,)),
            dma((nz,)),
            dma((nz // 2, ny)),
            dma((no // 2,)),
            dma((no // 2,)),
            dma((no // nt, nt // 2)),
            dma((no // nt, nt)),
            dma,
            dma((2,)),
        ],
        compiler_params=pltpu.CompilerParams(
            collective_id=0, has_side_effects=True, vmem_limit_bytes=60 * 2**20
        ),
    )(
        doc_vectors,
        query_states,
        proj_weight,
        document_token_length.reshape(-1, lanes),
        candidates,
    )


def solution(mesh, ny=4):
    no, nt = mesh.shape["doc"], mesh.shape["tok"]
    placed = (P("doc", "tok", None), P(), P("doc", "tok", None), P("doc"), P("doc", None))
    return jax.shard_map(
        functools.partial(on_device, ny, no // ny, nt),
        mesh=mesh, in_specs=placed, out_specs=P("doc", None), check_vma=False,
    )
```

```python
import functools

import jax
import jax.numpy as jnp
from jax import lax
from jax.experimental import pallas as pl
from jax.experimental.pallas import tpu as pltpu
from jax.sharding import PartitionSpec as P

MESH = pl.DeviceIdType.MESH
F32, BF16, I32 = jnp.float32, jnp.bfloat16, jnp.int32
NT = (((1,), (1,)), ((), ()))
GROUP = 2
LAG = 4


def iota(shape, dim):
    return lax.broadcasted_iota(I32, shape, dim)


def along(k):
    return (k + 1) // 2 if k % 2 else -(k // 2)


def schedule(ny, nz):
    own = [(m, 0) for m in range(nz // 2)]
    return own + [(m, p) for m in range(nz // 2) for p in range(1, ny)]


def kernel(
    ny, nz, nt, docs_hbm, qs_hbm, w_hbm, len_hbm, cand_hbm, out_ref,
    docs, docs2, qs, qrow, w, len_ref, cand_ref, ublk, pieces, qall, sorting, lists_out, lists_z, lists_in, near_lists, far_lists, combs, onehots, selects, ranks,
    sorted_q, raw, best, inbox, sums, table, table2,
    in_sem, a_send, a_recv, b_send, b_recv, v_send, v_recv, z_send, z_recv, y_send, d_send, d_recv, q_recv, l_send, l_recv, yl_send, yl_recv,
    m_send, m_recv, t_send, t_recv, s_sem,
):
    no = ny * nz
    d, t = lax.axis_index("doc"), lax.axis_index("tok")
    y, z, c = d // nz, d % nz, t % 2
    sibling = t + 1 - 2 * c
    nq, cands = cand_ref.shape
    ndocs = docs.shape[0]
    slots = docs.shape[1]
    shift = ndocs.bit_length() - 1
    per = qs.shape[1]
    qrows = nq * per * nt
    per_query = per * nt
    cap = lists_in.shape[2]
    order = schedule(ny, nz)
    groups = no // 2 // GROUP
    nx = nt // 2
    depth = nz // 2
    x, odd = t // 2, (z + c) % 2
    places = [[k for k in range(nz) if along(k) % 2 == side] for side in (0, 1)]

    pairs = ((qs_hbm, qs), (w_hbm, w), (cand_hbm, cand_ref), (len_hbm, len_ref), (docs_hbm, docs))
    loads = [pltpu.make_async_copy(src, dst, in_sem.at[i]) for i, (src, dst) in enumerate(pairs)]
    for load in loads:
        load.start()

    barrier = pltpu.get_barrier_semaphore()

    def greet(doc, tok):
        pl.semaphore_signal(barrier, inc=1, device_id={"doc": doc, "tok": tok}, device_id_type=MESH)

    for p in range(1, nz):
        greet(y * nz + (z + p) % nz, t)
    for p in range(1, ny):
        greet(((y + p) % ny) * nz + z, t)
    for p in range(1, nt):
        greet(d, (t + p) % nt)

    def send(src, dst, ssem, rsem, doc, tok):
        return pltpu.make_async_remote_copy(
            src_ref=src, dst_ref=dst, send_sem=ssem, recv_sem=rsem,
            device_id={"doc": doc, "tok": tok}, device_id_type=MESH,
        )

    def loop(first, last, do):
        def body(i, carry):
            do(i)
            return carry

        lax.fori_loop(first, last, body, 0)

    loads[0].wait()
    for q in range(nq):
        qrow[per * q : per * (q + 1)] = qs[q].astype(F32)
    loads[1].wait()
    proj = jnp.dot(qrow[...].astype(BF16), w[...], preferred_element_type=F32)
    unit = proj * lax.rsqrt(jnp.sum(proj * proj, axis=-1, keepdims=True) + 1e-06)
    ublk[0] = unit.astype(BF16)

    pl.semaphore_wait(barrier, nt - 1 + nz - 1 + ny - 1)

    def offset(k):
        return jnp.where(k % 2 == 1, (k + 1) // 2, -(k // 2))

    def send_z(k):
        to = (z + nz - offset(k)) % nz
        return send(ublk.at[0], ublk.at[k], z_send.at[k], z_recv.at[k], y * nz + to, t)

    def core_of(k):
        return (z + along(k) % 2) % 2

    def rank_of(k):
        return places[along(k) % 2].index(k)

    def to_core(k, p):
        return (x + p) % nx * 2 + core_of(k)

    def send_tok(k, p):
        return send(ublk.at[k], qall.at[rank_of(k), 0, t], a_send.at[k, p], a_recv.at[k, t], d, to_core(k, p))

    def rest(k):
        return qall.at[rank_of(k), pl.ds(1, ny - 1), t]

    def send_rest(k, p):
        return send(
            pieces.at[rank_of(k), pl.ds(1, ny - 1)], rest(k), b_send.at[k, p], b_recv.at[k, t], d, to_core(k, p)
        )

    def send_piece(k, p):
        return send(
            ublk.at[k], pieces.at[rank_of(k), ny - p], v_send.at[k, p], v_recv.at[k, ny - p],
            ((y + p) % ny) * nz + z, t,
        )

    def each_tok(k, make, do):
        pl.when(core_of(k) != c)(lambda: do(make(k, 0)))
        for p in range(1, nx):
            do(make(k, p))

    def go(copy):
        copy.start()

    def left(copy):
        copy.wait_send()

    for k in range(1, nz):
        send_z(k).start()
    def spread(k):
        each_tok(k, send_tok, go)
        if along(k) % 2:
            for p in range(1, ny):
                send_piece(k, p).start()

        @pl.when(core_of(k) == c)
        def _():
            qall[rank_of(k), 0, t] = ublk[k]

    spread(0)

    loads[2].wait()
    cand = cand_ref[...]
    shard_rows = []
    for q in range(nq):
        shard_rows.append((iota((no, cands), 0) == (cand[q : q + 1] >> shift)).astype(F32))
    before = (iota((cands, cands), 0) < iota((cands, cands), 1)).astype(BF16)
    prefix = jnp.dot(
        jnp.concatenate(shard_rows, axis=0).astype(BF16), before, preferred_element_type=F32
    )
    base = jnp.zeros((no, 1), F32)
    coded = jnp.zeros((2 * no, cap), F32)
    for q in range(nq):
        mine = shard_rows[q]
        rank = jnp.sum(mine * (prefix[no * q : no * (q + 1)] + base), axis=0, keepdims=True)
        base = base + jnp.sum(mine, axis=1, keepdims=True)
        number = rank.astype(I32)
        ranks[q] = (number % (cap // slots)) * slots + number // (cap // slots)
        onehots[q] = mine.astype(BF16)
        local = cand[q : q + 1] & (ndocs - 1)
        high = (local >> 8) + (ndocs >> 8) * q
        low = local & 255
        rank_rows = (iota((cap, cands), 0).astype(F32) == rank).astype(BF16)
        lhs = jnp.concatenate([mine * high.astype(F32), mine * low.astype(F32)], axis=0)
        coded = coded + lax.dot_general(lhs.astype(BF16), rank_rows, NT, preferred_element_type=F32)
    packed = coded[:no].astype(I32) * 256 + coded[no:].astype(I32)
    packed = jnp.where(iota((no, cap), 1).astype(F32) < base, packed, (nq - 1) * ndocs)
    for s in range(no):
        lists_out[s % nz, s // nz] = packed[s : s + 1]
    lists_z[z] = lists_out[z]

    def send_list(k):
        to = (z + nz + offset(k)) % nz
        return send(lists_out.at[to], lists_z.at[z], l_send.at[k], l_recv.at[z], y * nz + to, t)

    pl.when(c == z % 2)(lambda: loop(1, nz, lambda k: send_list(k).start()))

    row, col = iota((qrows, qrows), 0), iota((qrows, qrows), 1)
    from_row = ((row // per) % nt) * (per * nq) + (row // per_query) * per + row % per
    sorting[...] = (from_row == col).astype(BF16)
    pad = 128 - 3 * no
    for q in range(nq):
        mine = onehots[q]
        selects[q] = jnp.concatenate([mine, mine, mine, jnp.zeros((pad, cands), BF16)], axis=0)

    def relay(k):
        send_z(k).wait_recv()
        spread(k)

    def relay_rest(k):
        for p in range(1, ny):
            send_piece(k, ny - p).wait_recv()
        each_tok(k, send_rest, go)

        @pl.when(core_of(k) == c)
        def _():
            for p in range(1, ny):
                qall[rank_of(k), p, t] = pieces[rank_of(k), p]

    def owner(k, p):
        return ((y + p) % ny) * nz + (z + nz + offset(k)) % nz

    def send_y(m, p):
        return send(
            qall.at[m, 0], qall.at[m, ny - p], y_send.at[m, p], q_recv.at[m, ny - p], ((y + p) % ny) * nz + z, t
        )

    def send_row(m, p):
        o, to = owner(place(m), 0), (y + p) % ny
        slot = (ny - p) * depth + m
        return send(
            lists_z.at[o % nz, to], lists_in.at[slot], yl_send.at[m, p], yl_recv.at[slot], to * nz + z, t
        )

    def place(m):
        return jnp.where(odd == 0, places[0][m], places[1][m])

    def gathered(k, arrivals):
        for p in range(1, nt):
            src = (t + p) % nt
            send(ublk.at[0], ublk.at[0], d_send, arrivals.at[k, src], d, sibling).wait_recv()

    def gathered_rest(k):
        for p in range(1, nt):
            src = (t + p) % nt
            part = pieces.at[0, pl.ds(1, ny - 1)]
            send(part, part, d_send, b_recv.at[k, src], d, sibling).wait_recv()

    def forward(m):
        @pl.when(odd == 0)
        def _():
            gathered(places[0][m], a_recv)
            for p in range(1, ny):
                send_y(m, p).start()

    def forward_list(m):
        k = place(m)
        o = owner(k, 0)

        @pl.when(k != 0)
        def _():
            send(lists_z.at[o % nz], lists_z.at[o % nz], l_send.at[0], l_recv.at[o % nz], d, sibling).wait_recv()

        for p in range(1, ny):
            send_row(m, p).start()
        lists_in[m] = lists_z[o % nz, y]

    def row_arrived(m, p):
        slot = p * depth + m
        send(lists_in.at[slot], lists_in.at[slot], d_send, yl_recv.at[slot], d, sibling).wait_recv()

    def entry(g, i):
        m, k, p = jnp.int32(0), jnp.int32(0), jnp.int32(0)
        for n in range(groups):
            step_m, step_p = order[GROUP * n + i]
            m = jnp.where(g == n, step_m, m)
            k = jnp.where(g == n, place(step_m), k)
            p = jnp.where(g == n, step_p, p)
        return m, k, p, owner(k, p), p * depth + m

    def complete(g):
        for i in range(GROUP):
            m, k, p, _, _ = entry(g, i)

            @pl.when((odd == 0) & (p != 0))
            def _():
                send(qall.at[m, p], qall.at[m, p], d_send, q_recv.at[m, p], d, sibling).wait_recv()

            @pl.when((odd == 1) & (p == 0))
            def _():
                gathered(k, a_recv)

            @pl.when((odd == 1) & (p == 1))
            def _():
                gathered_rest(k)

    lane = iota((8, cap), 1)
    lanes = len_ref.shape[1]
    position = t * slots + lane % slots
    position2 = sibling * slots + lane % slots
    blocks = cap // slots

    def combine(slot):
        line = jnp.broadcast_to(lists_in[slot], (8, cap))
        doc_id = line & (ndocs - 1)
        length = jnp.zeros((8, cap), I32)
        for r in range(len_ref.shape[0]):
            found = jnp.take_along_axis(
                jnp.broadcast_to(len_ref[r : r + 1], (8, lanes)), doc_id % lanes, axis=1
            )
            length = jnp.where(doc_id // lanes == r, found, length)
        combs[slot] = (line >> shift) * 256 + length

    def merge(a, b, dist):
        keep = ((lane // dist) % 2 == 0)[None]
        a_back = pltpu.roll(a, cap - dist, 2)
        b_on = pltpu.roll(b, dist, 2)
        return jnp.maximum(jnp.where(keep, a, b_on), jnp.where(keep, a_back, b))

    window = nq // 2

    def starts(lists, o):
        first, extra = [], jnp.int32(0)
        for v in range(blocks):
            first.append(jnp.minimum((lists[o, 0, slots * v] >> shift) & (nq - 1), nq - window))
            last = (lists[o, 0, slots * v + slots - 1] >> shift) & (nq - 1)
            extra = extra + jnp.where(last - first[v] >= window, v, 0)
        return first, extra & (blocks - 1)

    def product(lists, o, query, v):
        picks = [lists[o, 0, slots * v + n] & (ndocs - 1) for n in range(slots)]
        out = []
        for source in (docs, docs2):
            matrix = jnp.concatenate([source[i] for i in picks], axis=0)
            out.append(lax.dot_general(query, matrix, NT, preferred_element_type=F32))
        return out

    def chosen(sims, h, whose, start, picked):
        block = sims[:, h * cap : (h + 1) * cap].reshape(window, per_query // 8, 8, cap)
        for q in range(window):
            here = block[q] if picked is None else jnp.where((whose == start + q)[None], block[q], picked)
            picked = here
        return picked

    def spread_comb(comb, v, h):
        return jnp.take_along_axis(comb, (2 * v + h) * blocks + lane // slots, axis=1)

    def rows_of(i, start):
        return jnp.concatenate([sorted_q[i, start + q] for q in range(window)], axis=0)

    def further(lists, o, i, comb, extra):
        sims = product(lists, o, rows_of(i, nq - window), extra)
        out = []
        for h in range(2):
            whose = spread_comb(comb, extra, h) >> 8
            out.append([chosen(part, h, whose, nq - window, None) for part in sims])
        return out

    def tile(lists, o, i, comb, first, past, v):
        sims = product(lists, o, rows_of(i, first[v]), v)
        out = []
        for h in range(2):
            here = spread_comb(comb, v, h)
            whose, until = here >> 8, here & 255
            mine = chosen(sims[0], h, whose, first[v], past[h][0])
            theirs = chosen(sims[1], h, whose, first[v], past[h][1])
            mine = jnp.where((position < until)[None], mine, F32(-1e30))
            theirs = jnp.where((position2 < until)[None], theirs, F32(-1e30))
            out.append(jnp.maximum(mine, theirs))
        return out

    def fold(leaf, v, dist):
        if dist == slots:
            return merge(*leaf(v), 1)
        return merge(fold(leaf, v, dist * 2), fold(leaf, v + dist // 2, dist * 2), dist)

    def put(j, value):
        best[j + 1] = value.reshape(per_query, cap)

    def kept(v):
        return raw[2 * v], raw[2 * v + 1]

    def compute(g, lists, skipped):
        put(GROUP * g - 1, fold(kept, 0, 2))
        for i in range(GROUP):
            m, _, p, _, _ = entry(g, i)
            mixed = qall[m, p].reshape(qrows, qall.shape[4])
            query = jnp.dot(sorting[...], mixed, preferred_element_type=F32).astype(BF16)
            sorted_q[i] = query.reshape(nq, per_query, query.shape[1])
        for i in range(GROUP):
            slot = entry(g, i)[4]
            comb = combs[slot]
            o = slot - skipped
            first, extra = starts(lists, o)
            past = further(lists, o, i, comb, extra)
            leaf = functools.partial(tile, lists, o, i, comb, first, past)
            if i < GROUP - 1:
                put(GROUP * g + i, fold(leaf, 0, 2))
            else:
                for v in range(blocks):
                    raw[2 * v], raw[2 * v + 1] = leaf(v)
        for i in range(GROUP):
            combine(entry(jnp.minimum(g + 1, groups - 1), i)[4])

    def send_best(j):
        return send(best.at[j + 1], inbox.at[j // nx, x], m_send.at[j], m_recv.at[j // nx, x], d, j % nx * 2 + c)

    def give_best(j):
        @pl.when((j >= 0) & (j % nx != x))
        def _():
            send_best(j).start()

    def target(m):
        j = x + nx * m
        o = jnp.int32(0)
        for i in range(GROUP):
            o = jnp.where(j % GROUP == i, entry(j // GROUP, i)[3], o)
        return o

    def send_sum(m, tp, o):
        return (
            (o == d) & (tp == t),
            send(sums.at[m], table.at[d], t_send.at[m, tp], t_recv, o, tp),
            pltpu.make_async_copy(sums.at[m], table.at[d], t_recv),
        )

    def reduce(m):
        total = best[x + nx * m + 1]
        for p in range(1, nx):
            src = (x + p) % nx
            send(inbox.at[m, src], inbox.at[m, src], d_send, m_recv.at[m, src], d, sibling).wait_recv()
            total = jnp.maximum(total, inbox[m, src])
        sums[m] = jnp.sum(total, axis=0, keepdims=True)
        o = target(m)

        def give(tp):
            mine, copy, keep = send_sum(m, tp, o)

            @pl.when(mine)
            def _():
                keep.start()

            @pl.when(jnp.logical_not(mine))
            def _():
                copy.start()

        loop(0, nt, give)

    share_docs = send(docs, docs2, d_send, d_recv, d, sibling)
    loads[3].wait()
    loads[4].wait()
    share_docs.start()
    for k in range(1, nz):
        relay(k)
    for m in range(nz // 2):
        forward_list(m)
    forward(0)
    near_smem = pltpu.make_async_copy(lists_in.at[pl.ds(0, depth)], near_lists, s_sem.at[0])
    far_smem = pltpu.make_async_copy(lists_in.at[pl.ds(depth, no // 2 - depth)], far_lists, s_sem.at[1])
    near_smem.start()
    for i in range(GROUP):
        combine(entry(0, i)[4])

    def step(g, lists, skipped):
        complete(g)
        compute(g, lists, skipped)
        for i in range(GROUP):
            give_best(GROUP * g + i - 1)

    near_groups = depth // GROUP
    for m in range(1, depth):
        if 2 * m - 1 < len(places[1]):
            relay_rest(places[1][2 * m - 2])
            relay_rest(places[1][2 * m - 1])
        forward(m)
        if m == depth - 1:
            for n in range(depth):
                for p in range(1, ny):
                    row_arrived(n, p)
            far_smem.start()
        if m == GROUP - 1:
            near_smem.wait()
            share_docs.wait_recv()
        if (m + 1) % GROUP == 0:
            step(jnp.int32((m + 1) // GROUP - 1), near_lists, 0)
    far_smem.wait()
    summing = [(nx * (m + 1) - 1) // GROUP + LAG for m in range(no // nt)]

    def far_step(g):
        step(g, far_lists, depth)
        for m, n in enumerate(summing):
            if n < groups:
                pl.when(g == n)(functools.partial(reduce, m))

    loop(near_groups, groups, far_step)
    put(no // 2 - 1, fold(kept, 0, 2))
    give_best(jnp.int32(no // 2 - 1))
    for m, n in enumerate(summing):
        if n >= groups:
            reduce(m)

    for k in range(nz):
        each_tok(k, send_tok, left)
        if along(k) % 2:
            each_tok(k, send_rest, left)
            for p in range(1, ny):
                send_piece(k, p).wait_send()
    for k in range(1, nz):
        send_z(k).wait_send()
    for m in range(nz // 2):
        for p in range(1, ny):
            pl.when(odd == 0)(lambda: send_y(m, p).wait_send())
            send_row(m, p).wait_send()
    share_docs.wait_send()
    pl.when(c == z % 2)(lambda: loop(1, nz, lambda k: send_list(k).wait_send()))

    def drained(j):
        @pl.when(j % nx != x)
        def _():
            send_best(j).wait_send()

    loop(0, no // 2, drained)

    def sums_left(i):
        mine, copy, _ = send_sum(i // nt, i % nt, target(i // nt))

        @pl.when(jnp.logical_not(mine))
        def _():
            copy.wait_send()

    loop(0, no, sums_left)

    send(table, table, d_send, t_recv, d, sibling).wait_recv()

    for s in range(no):
        table2[s : s + 1] = table[s]
    whole = table2[...]
    top = whole.astype(BF16).astype(F32)
    rest = whole - top
    middle = rest.astype(BF16).astype(F32)
    stacked = [top, middle, rest - middle]
    stacked.append(jnp.zeros((pad, cap), F32))
    turned = jnp.transpose(jnp.concatenate(stacked, axis=0)).astype(BF16)
    for q in range(nq):
        found = jnp.dot(turned, selects[q], preferred_element_type=F32)
        hit = iota((cap, cands), 0) == ranks[q]
        out_ref[q : q + 1] = jnp.sum(jnp.where(hit, found, F32(0.0)), axis=0, keepdims=True)


def on_device(ny, nz, nt, query_states, proj_weight, doc_vectors, document_token_length, candidates):
    nq, per, width = query_states.shape
    ndocs, slots, dim = doc_vectors.shape
    cands = candidates.shape[1]
    no = ny * nz
    cap = 2 * nq * cands // no
    rows = nq * per
    lanes = min(128, ndocs)
    dma = pltpu.SemaphoreType.DMA
    hbm = pl.BlockSpec(memory_space=pl.ANY)
    return pl.pallas_call(
        functools.partial(kernel, ny, nz, nt),
        out_shape=jax.ShapeDtypeStruct((nq, cands), F32),
        in_specs=[hbm] * 5,
        out_specs=pl.BlockSpec(memory_space=pltpu.VMEM),
        scratch_shapes=[
            pltpu.VMEM((ndocs, slots, dim), BF16),
            pltpu.VMEM((ndocs, slots, dim), BF16),
            pltpu.VMEM((nq, per, width), BF16),
            pltpu.VMEM((rows, width), F32),
            pltpu.VMEM((width, dim), BF16),
            pltpu.VMEM((ndocs // lanes, lanes), I32),
            pltpu.VMEM((nq, cands), I32),
            pltpu.VMEM((nz, rows, dim), BF16),
            pltpu.VMEM((nz // 2, ny, rows, dim), BF16),
            pltpu.VMEM((nz // 2, ny, nt, rows, dim), BF16),
            pltpu.VMEM((rows * nt, rows * nt), BF16),
            pltpu.VMEM((nz, ny, 1, cap), I32),
            pltpu.VMEM((nz, ny, 1, cap), I32),
            pltpu.VMEM((no // 2, 1, cap), I32),
            pltpu.SMEM((nz // 2, 1, cap), I32),
            pltpu.SMEM((no // 2 - nz // 2, 1, cap), I32),
            pltpu.VMEM((no // 2, 8, cap), I32),
            pltpu.VMEM((nq, no, cands), BF16),
            pltpu.VMEM((nq, 128, cands), BF16),
            pltpu.VMEM((nq, 1, cands), I32),
            pltpu.VMEM((GROUP, nq, per * nt, dim), BF16),
            pltpu.VMEM((slots, per * nt // 8, 8, cap), F32),
            pltpu.VMEM((no // 2 + 1, per * nt, cap), F32),
            pltpu.VMEM((no // nt, nt // 2, per * nt, cap), F32),
            pltpu.VMEM((no // nt, 1, cap), F32),
            pltpu.VMEM((no, 1, cap), F32),
            pltpu.VMEM((no, cap), F32),
            dma((5,)),
            dma((nz, nt // 2)),
            dma((nz, nt)),
            dma((nz, nt // 2)),
            dma((nz, nt)),
            dma((nz, ny)),
            dma((nz, ny)),
            dma((nz,)),
            dma((nz,)),
            dma((nz // 2, ny)),
            dma,
            dma,
            dma((nz // 2, ny)),
            dma((nz,)),
            dma((nz,)),
            dma((nz // 2, ny)),
            dma((no // 2,)),
            dma((no // 2,)),
            dma((no // nt, nt // 2)),
            dma((no // nt, nt)),
            dma,
            dma((2,)),
        ],
        compiler_params=pltpu.CompilerParams(
            collective_id=0, has_side_effects=True, vmem_limit_bytes=60 * 2**20
        ),
    )(
        doc_vectors,
        query_states,
        proj_weight,
        document_token_length.reshape(-1, lanes),
        candidates,
    )


def solution(mesh, ny=4):
    no, nt = mesh.shape["doc"], mesh.shape["tok"]
    placed = (P("doc", "tok", None), P(), P("doc", "tok", None), P("doc"), P("doc", None))
    return jax.shard_map(
        functools.partial(on_device, ny, no // ny, nt),
        mesh=mesh, in_specs=placed, out_specs=P("doc", None), check_vma=False,
    )
```

```python
import functools

import jax
import jax.numpy as jnp
from jax import lax
from jax.experimental import pallas as pl
from jax.experimental.pallas import tpu as pltpu
from jax.sharding import PartitionSpec as P

MESH = pl.DeviceIdType.MESH
F32, BF16, I32 = jnp.float32, jnp.bfloat16, jnp.int32
NT = (((1,), (1,)), ((), ()))
GROUP = 2
LAG = 8


def iota(shape, dim):
    return lax.broadcasted_iota(I32, shape, dim)


def along(k):
    return (k + 1) // 2 if k % 2 else -(k // 2)


def schedule(ny, nz):
    own = [(m, 0) for m in range(nz // 2)]
    return own + [(m, p) for m in range(nz // 2) for p in range(1, ny)]


def kernel(
    ny, nz, nt, docs_hbm, qs_hbm, w_hbm, len_hbm, cand_hbm, out_ref,
    docs, docs2, qs, qrow, w, len_ref, cand_ref, ublk, pieces, qall, sorting, lists_out, lists_z, lists_in, near_lists, far_lists, combs, onehots, selects, ranks,
    sorted_q, raw, best, inbox, sums, table, table2,
    in_sem, a_send, a_recv, b_send, b_recv, v_send, v_recv, z_send, z_recv, y_send, d_send, d_recv, q_recv, l_send, l_recv, yl_send, yl_recv,
    m_send, m_recv, t_send, t_recv, s_sem,
):
    no = ny * nz
    d, t = lax.axis_index("doc"), lax.axis_index("tok")
    y, z, c = d // nz, d % nz, t % 2
    sibling = t + 1 - 2 * c
    nq, cands = cand_ref.shape
    ndocs = docs.shape[0]
    slots = docs.shape[1]
    shift = ndocs.bit_length() - 1
    per = qs.shape[1]
    qrows = nq * per * nt
    per_query = per * nt
    cap = lists_in.shape[2]
    order = schedule(ny, nz)
    groups = no // 2 // GROUP
    nx = nt // 2
    depth = nz // 2
    x, odd = t // 2, (z + c) % 2
    places = [[k for k in range(nz) if along(k) % 2 == side] for side in (0, 1)]

    pairs = ((qs_hbm, qs), (w_hbm, w), (cand_hbm, cand_ref), (len_hbm, len_ref), (docs_hbm, docs))
    loads = [pltpu.make_async_copy(src, dst, in_sem.at[i]) for i, (src, dst) in enumerate(pairs)]
    for load in loads:
        load.start()

    barrier = pltpu.get_barrier_semaphore()

    def greet(doc, tok):
        pl.semaphore_signal(barrier, inc=1, device_id={"doc": doc, "tok": tok}, device_id_type=MESH)

    for p in range(1, nz):
        greet(y * nz + (z + p) % nz, t)
    for p in range(1, ny):
        greet(((y + p) % ny) * nz + z, t)
    for p in range(1, nt):
        greet(d, (t + p) % nt)

    def send(src, dst, ssem, rsem, doc, tok):
        return pltpu.make_async_remote_copy(
            src_ref=src, dst_ref=dst, send_sem=ssem, recv_sem=rsem,
            device_id={"doc": doc, "tok": tok}, device_id_type=MESH,
        )

    def loop(first, last, do):
        def body(i, carry):
            do(i)
            return carry

        lax.fori_loop(first, last, body, 0)

    loads[0].wait()
    for q in range(nq):
        qrow[per * q : per * (q + 1)] = qs[q].astype(F32)
    loads[1].wait()
    proj = jnp.dot(qrow[...].astype(BF16), w[...], preferred_element_type=F32)
    unit = proj * lax.rsqrt(jnp.sum(proj * proj, axis=-1, keepdims=True) + 1e-06)
    ublk[0] = unit.astype(BF16)

    pl.semaphore_wait(barrier, nt - 1 + nz - 1 + ny - 1)

    def offset(k):
        return jnp.where(k % 2 == 1, (k + 1) // 2, -(k // 2))

    def send_z(k):
        to = (z + nz - offset(k)) % nz
        return send(ublk.at[0], ublk.at[k], z_send.at[k], z_recv.at[k], y * nz + to, t)

    def core_of(k):
        return (z + along(k) % 2) % 2

    def rank_of(k):
        return places[along(k) % 2].index(k)

    def to_core(k, p):
        return (x + p) % nx * 2 + core_of(k)

    def send_tok(k, p):
        return send(ublk.at[k], qall.at[rank_of(k), 0, t], a_send.at[k, p], a_recv.at[k, t], d, to_core(k, p))

    def rest(k):
        return qall.at[rank_of(k), pl.ds(1, ny - 1), t]

    def send_rest(k, p):
        return send(
            pieces.at[rank_of(k), pl.ds(1, ny - 1)], rest(k), b_send.at[k, p], b_recv.at[k, t], d, to_core(k, p)
        )

    def send_piece(k, p):
        return send(
            ublk.at[k], pieces.at[rank_of(k), ny - p], v_send.at[k, p], v_recv.at[k, ny - p],
            ((y + p) % ny) * nz + z, t,
        )

    def each_tok(k, make, do):
        pl.when(core_of(k) != c)(lambda: do(make(k, 0)))
        for p in range(1, nx):
            do(make(k, p))

    def go(copy):
        copy.start()

    def left(copy):
        copy.wait_send()

    for k in range(1, nz):
        send_z(k).start()
    def spread(k):
        each_tok(k, send_tok, go)
        if along(k) % 2:
            for p in range(1, ny):
                send_piece(k, p).start()

        @pl.when(core_of(k) == c)
        def _():
            qall[rank_of(k), 0, t] = ublk[k]

    spread(0)

    loads[2].wait()
    cand = cand_ref[...]
    shard_rows = []
    for q in range(nq):
        shard_rows.append((iota((no, cands), 0) == (cand[q : q + 1] >> shift)).astype(F32))
    before = (iota((cands, cands), 0) < iota((cands, cands), 1)).astype(BF16)
    prefix = jnp.dot(
        jnp.concatenate(shard_rows, axis=0).astype(BF16), before, preferred_element_type=F32
    )
    base = jnp.zeros((no, 1), F32)
    coded = jnp.zeros((2 * no, cap), F32)
    for q in range(nq):
        mine = shard_rows[q]
        rank = jnp.sum(mine * (prefix[no * q : no * (q + 1)] + base), axis=0, keepdims=True)
        base = base + jnp.sum(mine, axis=1, keepdims=True)
        number = rank.astype(I32)
        ranks[q] = (number % (cap // slots)) * slots + number // (cap // slots)
        onehots[q] = mine.astype(BF16)
        local = cand[q : q + 1] & (ndocs - 1)
        high = (local >> 8) + (ndocs >> 8) * q
        low = local & 255
        rank_rows = (iota((cap, cands), 0).astype(F32) == rank).astype(BF16)
        lhs = jnp.concatenate([mine * high.astype(F32), mine * low.astype(F32)], axis=0)
        coded = coded + lax.dot_general(lhs.astype(BF16), rank_rows, NT, preferred_element_type=F32)
    packed = coded[:no].astype(I32) * 256 + coded[no:].astype(I32)
    packed = jnp.where(iota((no, cap), 1).astype(F32) < base, packed, (nq - 1) * ndocs)
    for s in range(no):
        lists_out[s % nz, s // nz] = packed[s : s + 1]
    lists_z[z] = lists_out[z]

    def send_list(k):
        to = (z + nz + offset(k)) % nz
        return send(lists_out.at[to], lists_z.at[z], l_send.at[k], l_recv.at[z], y * nz + to, t)

    pl.when(c == z % 2)(lambda: loop(1, nz, lambda k: send_list(k).start()))

    row, col = iota((qrows, qrows), 0), iota((qrows, qrows), 1)
    from_row = ((row // per) % nt) * (per * nq) + (row // per_query) * per + row % per
    sorting[...] = (from_row == col).astype(BF16)
    pad = 128 - 3 * no
    for q in range(nq):
        mine = onehots[q]
        selects[q] = jnp.concatenate([mine, mine, mine, jnp.zeros((pad, cands), BF16)], axis=0)

    def relay(k):
        send_z(k).wait_recv()
        spread(k)

    def relay_rest(k):
        for p in range(1, ny):
            send_piece(k, ny - p).wait_recv()
        each_tok(k, send_rest, go)

        @pl.when(core_of(k) == c)
        def _():
            for p in range(1, ny):
                qall[rank_of(k), p, t] = pieces[rank_of(k), p]

    def owner(k, p):
        return ((y + p) % ny) * nz + (z + nz + offset(k)) % nz

    def send_y(m, p):
        return send(
            qall.at[m, 0], qall.at[m, ny - p], y_send.at[m, p], q_recv.at[m, ny - p], ((y + p) % ny) * nz + z, t
        )

    def send_row(m, p):
        o, to = owner(place(m), 0), (y + p) % ny
        slot = (ny - p) * depth + m
        return send(
            lists_z.at[o % nz, to], lists_in.at[slot], yl_send.at[m, p], yl_recv.at[slot], to * nz + z, t
        )

    def place(m):
        return jnp.where(odd == 0, places[0][m], places[1][m])

    def gathered(k, arrivals):
        for p in range(1, nt):
            src = (t + p) % nt
            send(ublk.at[0], ublk.at[0], d_send, arrivals.at[k, src], d, sibling).wait_recv()

    def gathered_rest(k):
        for p in range(1, nt):
            src = (t + p) % nt
            part = pieces.at[0, pl.ds(1, ny - 1)]
            send(part, part, d_send, b_recv.at[k, src], d, sibling).wait_recv()

    def forward(m):
        @pl.when(odd == 0)
        def _():
            gathered(places[0][m], a_recv)
            for p in range(1, ny):
                send_y(m, p).start()

    def forward_list(m):
        k = place(m)
        o = owner(k, 0)

        @pl.when(k != 0)
        def _():
            send(lists_z.at[o % nz], lists_z.at[o % nz], l_send.at[0], l_recv.at[o % nz], d, sibling).wait_recv()

        for p in range(1, ny):
            send_row(m, p).start()
        lists_in[m] = lists_z[o % nz, y]

    def row_arrived(m, p):
        slot = p * depth + m
        send(lists_in.at[slot], lists_in.at[slot], d_send, yl_recv.at[slot], d, sibling).wait_recv()

    def entry(g, i):
        m, k, p = jnp.int32(0), jnp.int32(0), jnp.int32(0)
        for n in range(groups):
            step_m, step_p = order[GROUP * n + i]
            m = jnp.where(g == n, step_m, m)
            k = jnp.where(g == n, place(step_m), k)
            p = jnp.where(g == n, step_p, p)
        return m, k, p, owner(k, p), p * depth + m

    def complete(g):
        for i in range(GROUP):
            m, k, p, _, _ = entry(g, i)

            @pl.when((odd == 0) & (p != 0))
            def _():
                send(qall.at[m, p], qall.at[m, p], d_send, q_recv.at[m, p], d, sibling).wait_recv()

            @pl.when((odd == 1) & (p == 0))
            def _():
                gathered(k, a_recv)

            @pl.when((odd == 1) & (p == 1))
            def _():
                gathered_rest(k)

    lane = iota((8, cap), 1)
    lanes = len_ref.shape[1]
    position = t * slots + lane % slots
    position2 = sibling * slots + lane % slots
    blocks = cap // slots

    def combine(slot):
        line = jnp.broadcast_to(lists_in[slot], (8, cap))
        doc_id = line & (ndocs - 1)
        length = jnp.zeros((8, cap), I32)
        for r in range(len_ref.shape[0]):
            found = jnp.take_along_axis(
                jnp.broadcast_to(len_ref[r : r + 1], (8, lanes)), doc_id % lanes, axis=1
            )
            length = jnp.where(doc_id // lanes == r, found, length)
        combs[slot] = (line >> shift) * 256 + length

    def merge(a, b, dist):
        keep = ((lane // dist) % 2 == 0)[None]
        a_back = pltpu.roll(a, cap - dist, 2)
        b_on = pltpu.roll(b, dist, 2)
        return jnp.maximum(jnp.where(keep, a, b_on), jnp.where(keep, a_back, b))

    window = nq // 2

    def starts(lists, o):
        first, extra = [], jnp.int32(0)
        for v in range(blocks):
            first.append(jnp.minimum((lists[o, 0, slots * v] >> shift) & (nq - 1), nq - window))
            last = (lists[o, 0, slots * v + slots - 1] >> shift) & (nq - 1)
            extra = extra + jnp.where(last - first[v] >= window, v, 0)
        return first, extra & (blocks - 1)

    def product(lists, o, query, v):
        picks = [lists[o, 0, slots * v + n] & (ndocs - 1) for n in range(slots)]
        out = []
        for source in (docs, docs2):
            matrix = jnp.concatenate([source[i] for i in picks], axis=0)
            out.append(lax.dot_general(query, matrix, NT, preferred_element_type=F32))
        return out

    def chosen(sims, h, whose, start, picked):
        block = sims[:, h * cap : (h + 1) * cap].reshape(window, per_query // 8, 8, cap)
        for q in range(window):
            here = block[q] if picked is None else jnp.where((whose == start + q)[None], block[q], picked)
            picked = here
        return picked

    def spread_comb(comb, v, h):
        return jnp.take_along_axis(comb, (2 * v + h) * blocks + lane // slots, axis=1)

    def rows_of(i, start):
        return jnp.concatenate([sorted_q[i, start + q] for q in range(window)], axis=0)

    def further(lists, o, i, comb, extra):
        sims = product(lists, o, rows_of(i, nq - window), extra)
        out = []
        for h in range(2):
            whose = spread_comb(comb, extra, h) >> 8
            out.append([chosen(part, h, whose, nq - window, None) for part in sims])
        return out

    def tile(lists, o, i, comb, first, past, v):
        sims = product(lists, o, rows_of(i, first[v]), v)
        out = []
        for h in range(2):
            here = spread_comb(comb, v, h)
            whose, until = here >> 8, here & 255
            mine = chosen(sims[0], h, whose, first[v], past[h][0])
            theirs = chosen(sims[1], h, whose, first[v], past[h][1])
            mine = jnp.where((position < until)[None], mine, F32(-1e30))
            theirs = jnp.where((position2 < until)[None], theirs, F32(-1e30))
            out.append(jnp.maximum(mine, theirs))
        return out

    def fold(leaf, v, dist):
        if dist == slots:
            return merge(*leaf(v), 1)
        return merge(fold(leaf, v, dist * 2), fold(leaf, v + dist // 2, dist * 2), dist)

    def put(j, value):
        best[j + 1] = value.reshape(per_query, cap)

    def kept(v):
        return raw[2 * v], raw[2 * v + 1]

    def compute(g, lists, skipped):
        put(GROUP * g - 1, fold(kept, 0, 2))
        for i in range(GROUP):
            m, _, p, _, _ = entry(g, i)
            mixed = qall[m, p].reshape(qrows, qall.shape[4])
            query = jnp.dot(sorting[...], mixed, preferred_element_type=F32).astype(BF16)
            sorted_q[i] = query.reshape(nq, per_query, query.shape[1])
        for i in range(GROUP):
            slot = entry(g, i)[4]
            comb = combs[slot]
            o = slot - skipped
            first, extra = starts(lists, o)
            past = further(lists, o, i, comb, extra)
            leaf = functools.partial(tile, lists, o, i, comb, first, past)
            if i < GROUP - 1:
                put(GROUP * g + i, fold(leaf, 0, 2))
            else:
                for v in range(blocks):
                    raw[2 * v], raw[2 * v + 1] = leaf(v)
        for i in range(GROUP):
            combine(entry(jnp.minimum(g + 1, groups - 1), i)[4])

    def send_best(j):
        return send(best.at[j + 1], inbox.at[j // nx, x], m_send.at[j], m_recv.at[j // nx, x], d, j % nx * 2 + c)

    def give_best(j):
        @pl.when((j >= 0) & (j % nx != x))
        def _():
            send_best(j).start()

    def target(m):
        j = x + nx * m
        o = jnp.int32(0)
        for i in range(GROUP):
            o = jnp.where(j % GROUP == i, entry(j // GROUP, i)[3], o)
        return o

    def send_sum(m, tp, o):
        return (
            (o == d) & (tp == t),
            send(sums.at[m], table.at[d], t_send.at[m, tp], t_recv, o, tp),
            pltpu.make_async_copy(sums.at[m], table.at[d], t_recv),
        )

    def reduce(m):
        total = best[x + nx * m + 1]
        for p in range(1, nx):
            src = (x + p) % nx
            send(inbox.at[m, src], inbox.at[m, src], d_send, m_recv.at[m, src], d, sibling).wait_recv()
            total = jnp.maximum(total, inbox[m, src])
        sums[m] = jnp.sum(total, axis=0, keepdims=True)
        o = target(m)

        def give(tp):
            mine, copy, keep = send_sum(m, tp, o)

            @pl.when(mine)
            def _():
                keep.start()

            @pl.when(jnp.logical_not(mine))
            def _():
                copy.start()

        for tp in range(nt):
            give(tp)

    share_docs = send(docs, docs2, d_send, d_recv, d, sibling)
    loads[3].wait()
    loads[4].wait()
    share_docs.start()
    for k in range(1, nz):
        relay(k)
    for m in range(nz // 2):
        forward_list(m)
    forward(0)
    near_smem = pltpu.make_async_copy(lists_in.at[pl.ds(0, depth)], near_lists, s_sem.at[0])
    far_smem = pltpu.make_async_copy(lists_in.at[pl.ds(depth, no // 2 - depth)], far_lists, s_sem.at[1])
    near_smem.start()
    for i in range(GROUP):
        combine(entry(0, i)[4])

    def step(g, lists, skipped):
        complete(g)
        compute(g, lists, skipped)
        for i in range(GROUP):
            give_best(GROUP * g + i - 1)

    near_groups = depth // GROUP
    for m in range(1, depth):
        if 2 * m - 1 < len(places[1]):
            relay_rest(places[1][2 * m - 2])
            relay_rest(places[1][2 * m - 1])
        forward(m)
        if m == depth - 1:
            for n in range(depth):
                for p in range(1, ny):
                    row_arrived(n, p)
            far_smem.start()
        if m == GROUP - 1:
            near_smem.wait()
            share_docs.wait_recv()
        if (m + 1) % GROUP == 0:
            step(jnp.int32((m + 1) // GROUP - 1), near_lists, 0)
    far_smem.wait()
    summing = [(nx * (m + 1) - 1) // GROUP + LAG for m in range(no // nt)]

    def far_step(g):
        step(g, far_lists, depth)
        for m, n in enumerate(summing):
            if n < groups:
                pl.when(g == n)(functools.partial(reduce, m))

    loop(near_groups, groups, far_step)
    put(no // 2 - 1, fold(kept, 0, 2))
    give_best(jnp.int32(no // 2 - 1))
    for m, n in enumerate(summing):
        if n >= groups:
            reduce(m)

    for k in range(nz):
        each_tok(k, send_tok, left)
        if along(k) % 2:
            each_tok(k, send_rest, left)
            for p in range(1, ny):
                send_piece(k, p).wait_send()
    for k in range(1, nz):
        send_z(k).wait_send()
    for m in range(nz // 2):
        for p in range(1, ny):
            pl.when(odd == 0)(lambda: send_y(m, p).wait_send())
            send_row(m, p).wait_send()
    share_docs.wait_send()
    pl.when(c == z % 2)(lambda: loop(1, nz, lambda k: send_list(k).wait_send()))

    def drained(j):
        @pl.when(j % nx != x)
        def _():
            send_best(j).wait_send()

    loop(0, no // 2, drained)

    def sums_left(i):
        mine, copy, _ = send_sum(i // nt, i % nt, target(i // nt))

        @pl.when(jnp.logical_not(mine))
        def _():
            copy.wait_send()

    loop(0, no, sums_left)

    send(table, table, d_send, t_recv, d, sibling).wait_recv()

    for s in range(no):
        table2[s : s + 1] = table[s]
    whole = table2[...]
    top = whole.astype(BF16).astype(F32)
    rest = whole - top
    middle = rest.astype(BF16).astype(F32)
    stacked = [top, middle, rest - middle]
    stacked.append(jnp.zeros((pad, cap), F32))
    turned = jnp.transpose(jnp.concatenate(stacked, axis=0)).astype(BF16)
    for q in range(nq):
        found = jnp.dot(turned, selects[q], preferred_element_type=F32)
        hit = iota((cap, cands), 0) == ranks[q]
        out_ref[q : q + 1] = jnp.sum(jnp.where(hit, found, F32(0.0)), axis=0, keepdims=True)


def on_device(ny, nz, nt, query_states, proj_weight, doc_vectors, document_token_length, candidates):
    nq, per, width = query_states.shape
    ndocs, slots, dim = doc_vectors.shape
    cands = candidates.shape[1]
    no = ny * nz
    cap = 2 * nq * cands // no
    rows = nq * per
    lanes = min(128, ndocs)
    dma = pltpu.SemaphoreType.DMA
    hbm = pl.BlockSpec(memory_space=pl.ANY)
    return pl.pallas_call(
        functools.partial(kernel, ny, nz, nt),
        out_shape=jax.ShapeDtypeStruct((nq, cands), F32),
        in_specs=[hbm] * 5,
        out_specs=pl.BlockSpec(memory_space=pltpu.VMEM),
        scratch_shapes=[
            pltpu.VMEM((ndocs, slots, dim), BF16),
            pltpu.VMEM((ndocs, slots, dim), BF16),
            pltpu.VMEM((nq, per, width), BF16),
            pltpu.VMEM((rows, width), F32),
            pltpu.VMEM((width, dim), BF16),
            pltpu.VMEM((ndocs // lanes, lanes), I32),
            pltpu.VMEM((nq, cands), I32),
            pltpu.VMEM((nz, rows, dim), BF16),
            pltpu.VMEM((nz // 2, ny, rows, dim), BF16),
            pltpu.VMEM((nz // 2, ny, nt, rows, dim), BF16),
            pltpu.VMEM((rows * nt, rows * nt), BF16),
            pltpu.VMEM((nz, ny, 1, cap), I32),
            pltpu.VMEM((nz, ny, 1, cap), I32),
            pltpu.VMEM((no // 2, 1, cap), I32),
            pltpu.SMEM((nz // 2, 1, cap), I32),
            pltpu.SMEM((no // 2 - nz // 2, 1, cap), I32),
            pltpu.VMEM((no // 2, 8, cap), I32),
            pltpu.VMEM((nq, no, cands), BF16),
            pltpu.VMEM((nq, 128, cands), BF16),
            pltpu.VMEM((nq, 1, cands), I32),
            pltpu.VMEM((GROUP, nq, per * nt, dim), BF16),
            pltpu.VMEM((slots, per * nt // 8, 8, cap), F32),
            pltpu.VMEM((no // 2 + 1, per * nt, cap), F32),
            pltpu.VMEM((no // nt, nt // 2, per * nt, cap), F32),
            pltpu.VMEM((no // nt, 1, cap), F32),
            pltpu.VMEM((no, 1, cap), F32),
            pltpu.VMEM((no, cap), F32),
            dma((5,)),
            dma((nz, nt // 2)),
            dma((nz, nt)),
            dma((nz, nt // 2)),
            dma((nz, nt)),
            dma((nz, ny)),
            dma((nz, ny)),
            dma((nz,)),
            dma((nz,)),
            dma((nz // 2, ny)),
            dma,
            dma,
            dma((nz // 2, ny)),
            dma((nz,)),
            dma((nz,)),
            dma((nz // 2, ny)),
            dma((no // 2,)),
            dma((no // 2,)),
            dma((no // nt, nt // 2)),
            dma((no // nt, nt)),
            dma,
            dma((2,)),
        ],
        compiler_params=pltpu.CompilerParams(
            collective_id=0, has_side_effects=True, vmem_limit_bytes=60 * 2**20
        ),
    )(
        doc_vectors,
        query_states,
        proj_weight,
        document_token_length.reshape(-1, lanes),
        candidates,
    )


def solution(mesh, ny=4):
    no, nt = mesh.shape["doc"], mesh.shape["tok"]
    placed = (P("doc", "tok", None), P(), P("doc", "tok", None), P("doc"), P("doc", None))
    return jax.shard_map(
        functools.partial(on_device, ny, no // ny, nt),
        mesh=mesh, in_specs=placed, out_specs=P("doc", None), check_vma=False,
    )
```
